32 devices in a mesh: cmp: 4 (over y, x), tgt: 8 (over z, core).
Axes of the slice: x: 2, y: 2, z: 4, core: 2. Of those that a mesh axis runs over, the one named last changes fastest.
Arguments:
- affinity: bfloat16 [8192, 12288], P('cmp', 'tgt'), may hold values from -6 to 6
- comp_vectors: bfloat16 [8192, 2048], P('cmp'), may hold values from -0.0625 to 0.0625
- targ_vectors: bfloat16 [12288, 2048], P('tgt'), may hold values from -0.0546875 to 0.0546875
- comp_values: float32 [2048], P('cmp'), may hold values from 0.05 to 4
- targ_values: float32 [2048], P('tgt'), may hold values from 0.05 to 4
Outputs:
- predicted: float32 [8192, 12288], P('cmp', 'tgt')
The draws below stay inside these ranges and needn't reach their ends.
All inputs are finite; a program needn't handle non-finite values.
Results may differ from the reference program's by a relative error of at most 0.0037.
Values may be sent and summed in bfloat16 or wider, within the bound.
No kernel may reach another device: no remote copies, remote signals or barrier semaphores. Data moves between devices by JAX's collectives and lax.ppermute only.
A program may use at most 128 MiB of HBM per device.

```python
import math
import jax
import jax.numpy as jnp
from jax import lax

NT = 12288
KT = 2048
KC = 2048
NC = 8192


def level_of(key, extent, cuts, least, top_value):
    gain, own = 1.0, jax.random.fold_in(key, 6)
    for dim, blocks in cuts:
        steps = jnp.exp(jax.random.uniform(jax.random.fold_in(own, dim), (blocks,), jnp.float32, least / len(cuts), top_value / len(cuts)))
        gain = gain * jnp.repeat(steps, extent[dim] // blocks).reshape([-1 if axis == dim else 1 for axis in range(len(extent))])
    return gain


def noise(own_key, dims, width, bound, shards=(), kind=jnp.bfloat16):
    level = level_of(own_key, dims, shards, -0.22, 0.18) if shards else 1.0
    array = jax.random.normal(own_key, dims, jnp.float32) * width * level
    return jnp.minimum(jnp.maximum(array, -bound), bound).astype(kind)


def setup_inputs(seed: int = 0) -> dict:
    arg_keys = jax.random.split(jax.random.key(seed), 6)
    affinity = noise(arg_keys[0], (NC, NT), 1.0, 6.0, ((0, 4), (1, 8)))
    comp_vectors = noise(arg_keys[1], (NC, KC), NC ** -0.5, 0.0625, ((0, 4),))
    targ_vectors = noise(arg_keys[2], (NT, KT), NT ** -0.5, 0.0546875, ((0, 8),))
    comp_values = jnp.clip(jnp.exp(math.log(4.0) - 4.3820266 * jax.random.uniform(arg_keys[3], (KC,), jnp.float32) ** level_of(arg_keys[3], (KC,), ((0, 4),), -0.2, 0.2)), 0.05, 4.0)
    targ_values = jnp.clip(jnp.exp(math.log(4.0) - 4.3820266 * jax.random.uniform(arg_keys[4], (KT,), jnp.float32) ** level_of(arg_keys[4], (KT,), ((0, 8),), -0.2, 0.2)), 0.05, 4.0)
    return {"affinity": affinity, "comp_vectors": comp_vectors, "targ_vectors": targ_vectors, "comp_values": comp_values, "targ_values": targ_values}


def reference(affinity, comp_vectors, targ_vectors, comp_values, targ_values):
    half = jnp.dot(affinity, targ_vectors, preferred_element_type=jnp.float32)
    coeffs = jnp.dot(comp_vectors.astype(jnp.float32).T, half, precision=lax.Precision.HIGHEST, preferred_element_type=jnp.float32)
    scaled = (coeffs / (comp_values[:, None] * targ_values[None, :] + 0.25)).astype(jnp.bfloat16)
    mapped = jnp.dot(comp_vectors, scaled, preferred_element_type=jnp.float32).astype(jnp.bfloat16)
    return jnp.dot(mapped, targ_vectors.T, preferred_element_type=jnp.float32)
```

```python
import functools

import jax
import jax.numpy as jnp
from jax import lax
from jax.experimental import pallas as pl
from jax.experimental.pallas import tpu as pltpu
from jax.sharding import PartitionSpec as P

F32, BF16, F16 = jnp.float32, jnp.bfloat16, jnp.float16
VMEM = 48 * 1024 * 1024
NT_DIMS = (((1,), (1,)), ((), ()))


def dot_nt(a, b):
    return lax.dot_general(a, b, NT_DIMS, preferred_element_type=F32)


def call(kernel, name, grid, idx, in_specs, args, out_spec, out_shape, scratch, flops, nbytes, aliases=None):
    return pl.pallas_call(
        kernel,
        name=name,
        out_shape=out_shape,
        grid_spec=pltpu.PrefetchScalarGridSpec(
            num_scalar_prefetch=1, grid=grid, in_specs=in_specs, out_specs=out_spec, scratch_shapes=scratch
        ),
        input_output_aliases=aliases or {},
        cost_estimate=pl.CostEstimate(flops=flops, bytes_accessed=nbytes, transcendentals=0),
        compiler_params=pltpu.CompilerParams(vmem_limit_bytes=VMEM),
    )(idx, *args)


def first_product(aff, vt, idx, k, chunks, width, add=None):
    rows, depth = aff.shape
    nq = idx.shape[0]
    tile = 256

    def kernel(s, y, *refs):
        vts, rest = refs[:nq], refs[nq:]
        out, wide = rest[-2:]

        @pl.when(pl.program_id(0) == 0)
        def _():
            for q in range(nq):
                wide[q * width : (q + 1) * width, :] = vts[q][...].T

        acc = dot_nt(wide[...], y[...])
        if add is not None:
            acc = acc + rest[0][...].astype(F32)
        out[...] = acc.astype(out.dtype)

    in_specs = [pl.BlockSpec((tile, depth), lambda i, s: (i, 0))]
    in_specs += [pl.BlockSpec((depth, width), functools.partial(lambda q, i, s: (0, s[q] * chunks + k), q)) for q in range(nq)]
    args = [aff] + [vt] * nq
    if add is not None:
        in_specs.append(pl.BlockSpec((nq * width, tile), lambda i, s: (0, i)))
        args.append(add)
    return call(
        kernel, "half", (rows // tile,), idx, in_specs, args,
        pl.BlockSpec((nq * width, tile), lambda i, s: (0, i)),
        jax.ShapeDtypeStruct((nq * width, rows), BF16),
        [pltpu.VMEM((nq * width, depth), BF16)],
        2 * rows * depth * nq * width, 2 * rows * depth + 2 * nq * width * (rows + depth),
    )


def second_product(half, vc, idx, block, scale, dtype):
    wide, rows = half.shape
    n = idx.shape[0]
    tile = min(256, block)
    sub = block // tile

    def kernel(s, h, v, out):
        acc = jnp.dot(h[...], v[...], preferred_element_type=F32)
        out[...] = (acc * scale).astype(out.dtype)

    return call(
        kernel, "coeffs", (n * sub,), idx,
        [
            pl.BlockSpec((wide, rows), lambda j, s: (0, 0)),
            pl.BlockSpec((rows, tile), lambda j, s: (0, s[j // sub] * sub + j % sub)),
        ],
        [half, vc],
        pl.BlockSpec((wide, tile), lambda j, s: (0, j)),
        jax.ShapeDtypeStruct((wide, n * block), dtype),
        [],
        2 * wide * rows * n * block, 2 * wide * rows + 2 * rows * n * block + 4 * wide * n * block,
    )


def third_product(vc, near, far, idx, block):
    rows, depth = vc.shape
    wide, cols = near.shape
    n = cols // block
    tile = 256

    def kernel(s, v, a, b, out):
        acc = jnp.zeros(out.shape, F32)
        for p in range(2 * n):
            piece = (a if p < n else b)[:, (p % n) * block : (p % n + 1) * block]
            acc += dot_nt(v[:, pl.ds(pl.multiple_of(s[p] * block, block), block)], piece)
        out[...] = acc.astype(out.dtype)

    return call(
        kernel, "mapped", (rows // tile,), idx,
        [
            pl.BlockSpec((tile, depth), lambda i, s: (i, 0)),
            pl.BlockSpec((wide, cols), lambda i, s: (0, 0)),
            pl.BlockSpec((wide, cols), lambda i, s: (0, 0)),
        ],
        [vc, near, far],
        pl.BlockSpec((tile, wide), lambda i, s: (i, 0)),
        jax.ShapeDtypeStruct((rows, wide), BF16),
        [],
        2 * rows * depth * wide, 2 * rows * depth + 2 * wide * depth + 2 * rows * wide,
    )


def last_product(own, other, vt, idx, k, block, width, before):
    rows, wide = own.shape
    depth = vt.shape[0]
    nq = idx.shape[0]
    tile = 256

    def kernel(s, m, r, v, *rest):
        out, cols, sems = rest[-3:]

        @pl.when(pl.program_id(0) == 0)
        def _():
            copies = []
            for q in range(nq):
                at = pl.multiple_of(s[q] * block + k * width, width)
                copies.append(pltpu.make_async_copy(v.at[:, pl.ds(at, width)], cols.at[:, pl.ds(q * width, width)], sems.at[q]))
            for copy in copies:
                copy.start()
            for copy in copies:
                copy.wait()

        acc = dot_nt(jnp.concatenate([m[...], r[...]], axis=1), cols[...])
        if before is not None:
            acc = acc + rest[0][...]
        out[...] = acc

    in_specs = [
        pl.BlockSpec((tile, wide), lambda i, s: (i, 0)),
        pl.BlockSpec((tile, wide), lambda i, s: (i, 0)),
        pl.BlockSpec(memory_space=pl.ANY),
    ]
    args = [own, other, vt]
    aliases = None
    if before is not None:
        in_specs.append(pl.BlockSpec((tile, depth), lambda i, s: (i, 0)))
        args.append(before)
        aliases = {4: 0}
    return call(
        kernel, "predicted", (rows // tile,), idx, in_specs, args,
        pl.BlockSpec((tile, depth), lambda i, s: (i, 0)),
        jax.ShapeDtypeStruct((rows, depth), F32),
        [pltpu.VMEM((depth, 2 * wide), BF16), pltpu.SemaphoreType.DMA((nq,))],
        4 * rows * depth * wide, 4 * rows * wide + 4 * rows * depth * (1 if before is None else 2) + 4 * depth * wide,
        aliases,
    )


def shards(nc, nt, affinity, comp_vectors, targ_vectors, comp_values, targ_values):
    cbits, tbits = nc.bit_length() - 1, nt.bit_length() - 2
    orders = (list(range(cbits)), list(reversed(range(cbits))))
    iblock, jblock = comp_vectors.shape[1] // nc, targ_vectors.shape[1] // nt
    chunks = 2 if jblock % 256 == 0 else 1
    width = jblock // chunks
    at_c, at_t = lax.axis_index("cmp"), lax.axis_index("tgt")

    def offset(position, order):
        return sum(((position >> (len(order) - 1 - t)) & 1) << bit for t, bit in enumerate(order))

    even = jnp.array([offset(p, orders[0]) for p in range(nc)], jnp.int32)
    odd = jnp.array([offset(p, orders[1]) for p in range(nc)], jnp.int32)
    c_blocks = jnp.where(at_t % 2 == 0, even, odd) ^ at_c
    keep = jnp.array([offset(q, range(1, tbits + 1)) for q in range(nt // 2)], jnp.int32) ^ at_t
    give = keep ^ 1

    def swap_c(x, t):
        pairs = [(c * nt + i, (c ^ (1 << orders[i % 2][t])) * nt + i) for c in range(nc) for i in range(nt)]
        return lax.ppermute(x, ("cmp", "tgt"), pairs)

    def swap_t(x, bit):
        return lax.ppermute(x, "tgt", [(i, i ^ (1 << bit)) for i in range(nt)])

    bound = 6 * 0.0625 * 0.0546875 * affinity.shape[0] * nc * affinity.shape[1] * nt
    scale = 1.0
    while bound * scale > 65000:
        scale *= 0.5

    sent = [first_product(affinity, targ_vectors, give, k, chunks, width) for k in range(chunks)]
    came = [swap_t(x, 0) for x in sent]
    out = None
    pieces = []
    for k in range(chunks):
        half = first_product(affinity, targ_vectors, keep, k, chunks, width, came[k])
        far = swap_c(second_product(half, comp_vectors, c_blocks[nc // 2 :], iblock, scale, F32).astype(F16), 0)
        near = second_product(half, comp_vectors, c_blocks[: nc // 2], iblock, scale, F32)
        pieces.append((near, far))
    scaled = []
    for k in range(chunks):
        near, far = pieces[k]
        total = near + far.astype(F32)
        for t in range(1, cbits):
            n = total.shape[1] // 2
            total = total[:, :n] + swap_c(total[:, n:].astype(F16), t).astype(F32)
        for t in range(tbits):
            n = total.shape[0] // 2
            total = total[:n] + swap_t(total[n:].astype(F16), 1 + t).astype(F32)
        lt = targ_values[k * width : (k + 1) * width]
        scaled.append((total * (1 / scale) / (lt[:, None] * comp_values[None, :] + 0.25)).astype(BF16))
    for k in range(chunks):
        part = scaled[k]
        for t in reversed(range(tbits)):
            part = jnp.concatenate([part, swap_t(part, 1 + t)], axis=0)
        for t in reversed(range(1, cbits)):
            part = jnp.concatenate([part, swap_c(part, t)], axis=1)
        own = third_product(comp_vectors, part, swap_c(part, 0), c_blocks, iblock)
        other = swap_t(own, 0)
        out = last_product(own, other, targ_vectors, jnp.concatenate([keep, give]), k, jblock, width, out)
    return out


def solution(mesh):
    in_specs = (P("cmp", "tgt"), P("cmp", None), P("tgt", None), P("cmp"), P("tgt"))
    out_specs = P("cmp", "tgt")
    body = functools.partial(shards, mesh.shape["cmp"], mesh.shape["tgt"])
    return jax.shard_map(body, mesh=mesh, in_specs=in_specs, out_specs=out_specs, check_vma=False)
```

```python
import functools

import jax
import jax.numpy as jnp
from jax import lax
from jax.experimental import pallas as pl
from jax.experimental.pallas import tpu as pltpu
from jax.sharding import PartitionSpec as P

F32, BF16, F16 = jnp.float32, jnp.bfloat16, jnp.float16
LIMIT = 10 * 1024 * 1024
TILE = 512
IN_VMEM = pl.BlockSpec(memory_space=pltpu.VMEM)
IN_SMEM = pl.BlockSpec(memory_space=pltpu.SMEM)
IN_HBM = pl.BlockSpec(memory_space=pltpu.HBM)


def stay(x):
    return pltpu.with_memory_space_constraint(x, pltpu.VMEM)


def leave(x):
    return pltpu.with_memory_space_constraint(x, pltpu.HBM)


def dot_nn(a, b):
    return jnp.dot(a, b, preferred_element_type=F32)


def dot_nt(a, b):
    return lax.dot_general(a, b, (((1,), (1,)), ((), ())), preferred_element_type=F32)


def tiles(n):
    return [slice(i, min(i + TILE, n)) for i in range(0, n, TILE)]


def call(kernel, name, in_specs, args, out_specs, out_shape, scratch, flops):
    return pl.pallas_call(
        kernel,
        name=name,
        in_specs=in_specs,
        out_specs=out_specs,
        out_shape=out_shape,
        scratch_shapes=scratch,
        cost_estimate=pl.CostEstimate(flops=flops // 100, bytes_accessed=0, transcendentals=0),
        compiler_params=pltpu.CompilerParams(vmem_limit_bytes=LIMIT),
    )(*args)


def column_copies(idx, source, target, block, start, width, sem):
    found = []
    for q in range(target.shape[1] // width):
        at = pl.multiple_of(idx[q] * block + start, width)
        found.append(pltpu.make_async_copy(source.at[:, pl.ds(at, width)], target.at[:, pl.ds(q * width, width)], sem.at[q]))
    return found


def give_product(aff, vt, give, keep, chunks, block, width):
    depth, n = vt.shape[0], give.shape[0]
    rows, wide = aff.shape[0], n * width
    spans = tiles(rows)

    def kernel(*refs):
        s_give, s_keep, a, v, *outs = refs[: 4 + chunks]
        y, kept, given, y_sem, v_sem = refs[4 + chunks :]
        moves = [column_copies(s, v, to.at[k], block, k * width, width, v_sem.at[i, k])
                 for i, (s, to) in enumerate(((s_give, given), (s_keep, kept))) for k in range(chunks)]
        loads = [pltpu.make_async_copy(a.at[s, :], y.at[s, :], y_sem.at[i]) for i, s in enumerate(spans)]
        for move in moves[0] + loads + sum(moves[1:], []):
            move.start()
        for k in range(chunks):
            for move in moves[k]:
                move.wait()
            for i, s in enumerate(spans):
                if k == 0:
                    loads[i].wait()
                outs[k][:, s] = dot_nn(y[s, :], given[k]).astype(BF16).T
        for move in sum(moves[chunks:], []):
            move.wait()

    columns = pltpu.VMEM((chunks, depth, wide), BF16)
    out_shape = [jax.ShapeDtypeStruct((wide, rows), BF16)] * chunks + [pltpu.VMEM(aff.shape, BF16), columns]
    scratch = [columns, pltpu.SemaphoreType.DMA((len(spans),)), pltpu.SemaphoreType.DMA((2, chunks, n))]
    *sent, y, kept = call(
        kernel, "give", [IN_SMEM] * 2 + [IN_HBM] * 2, [give, keep, leave(aff), leave(vt)],
        [IN_VMEM] * len(out_shape), out_shape, scratch, 2 * rows * depth * wide * chunks,
    )
    return sent, y, kept


def keep_product(y, kept, vc, order, block):
    rows, depth = y.shape
    chunks, _, wide = kept.shape
    n = order.shape[0]

    def kernel(s, a, c, v, *refs):
        outs, w, sem = refs[:chunks], refs[chunks], refs[chunks + 1]
        moves = column_copies(s, v, w, block, 0, block, sem)
        for move in moves[n // 2 :] + moves[: n // 2]:
            move.start()
        for k in range(chunks):
            for t in tiles(rows):
                outs[k][:, t] = dot_nn(a[t, :], c[k]).T
        for move in moves:
            move.wait()

    out_shape = [pltpu.VMEM((wide, rows), F32)] * chunks + [pltpu.VMEM(vc.shape, BF16)]
    *halves, w = call(
        kernel, "keep", [IN_SMEM, IN_VMEM, IN_VMEM, IN_HBM], [order, stay(y), stay(kept), leave(vc)],
        [IN_VMEM] * len(out_shape), out_shape, [pltpu.SemaphoreType.DMA((n,))], 2 * rows * depth * wide * chunks,
    )
    return halves, w


def far_product(mine, came, vc, scale):
    wide, rows = mine.shape
    total = vc.shape[1]

    def kernel(h, r, w, half, out):
        half[...] = (h[...] + r[...].astype(F32)).astype(BF16)
        for t in tiles(total // 2):
            out[:, t] = dot_nn(half[...], w[:, t.start + total // 2 : t.stop + total // 2]) * scale

    out_shape = [pltpu.VMEM((wide, rows), BF16), jax.ShapeDtypeStruct((wide, total // 2), F32)]
    return call(
        kernel, "far", [IN_VMEM] * 3, [stay(mine), stay(came), stay(vc)], [IN_VMEM] * 2, out_shape, [], wide * rows * total
    )


def near_product(half, vc, scale):
    wide, rows = half.shape
    total = vc.shape[1]

    def kernel(h, w, out):
        for t in tiles(total // 2):
            out[:, t] = dot_nn(h[...], w[:, t]) * scale

    return call(
        kernel, "near", [IN_VMEM] * 2, [stay(half), stay(vc)], IN_VMEM, jax.ShapeDtypeStruct((wide, total // 2), F32), [],
        wide * rows * total,
    )


def mapped_product(vc, near, far, vt, idx, k, block, width):
    rows, total = vc.shape
    wide = near.shape[0]
    n = idx.shape[0]

    def kernel(s, w, a, b, v, out, cols, sem):
        moves = column_copies(s, v, cols, block, k * width, width, sem)
        for move in moves:
            move.start()
        for t in tiles(rows):
            out[t, :] = (dot_nt(w[t, : total // 2], a[...]) + dot_nt(w[t, total // 2 :], b[...])).astype(BF16)
        for move in moves:
            move.wait()

    out_shape = [jax.ShapeDtypeStruct((rows, wide), BF16), pltpu.VMEM((vt.shape[0], 2 * wide), BF16)]
    return call(
        kernel, "mapped", [IN_SMEM] + [IN_VMEM] * 3 + [IN_HBM], [idx, stay(vc), stay(near), stay(far), leave(vt)],
        [IN_VMEM] * 2, out_shape, [pltpu.SemaphoreType.DMA((n,))], 2 * rows * total * wide,
    )


def last_product(own, other, cols, before, last):
    rows, wide = own.shape
    depth = cols.shape[0]
    spans = [slice(i, i + 256) for i in range(0, rows, 256)]

    def kernel(m, r, c, *refs):
        part = lambda s: dot_nt(m[s, :], c[:, :wide]) + dot_nt(r[s, :], c[:, wide:])
        if not last:
            for s in spans:
                refs[-1][s, :] = part(s) + (0.0 if before is None else refs[0][s, :])
            return
        out, held, sem = refs[-3:]
        moves = [pltpu.make_async_copy(held.at[i % 2], out.at[s, :], sem.at[i % 2]) for i, s in enumerate(spans)]
        for i, s in enumerate(spans):
            if i >= 2:
                moves[i - 2].wait()
            held[i % 2] = part(s) + (0.0 if before is None else refs[0][s, :])
            moves[i].start()
        for move in moves[-2:]:
            move.wait()

    args = [stay(own), stay(other), stay(cols)] + ([] if before is None else [stay(before)])
    shape = (rows, depth)
    scratch = [pltpu.VMEM((2, 256, depth), F32), pltpu.SemaphoreType.DMA((2,))] if last else []
    return call(
        kernel, "predicted", [IN_VMEM] * len(args), args, IN_HBM if last else IN_VMEM,
        jax.ShapeDtypeStruct(shape, F32) if last else pltpu.VMEM(shape, F32), scratch, 4 * rows * depth * wide,
    )


def shards(nc, nt, affinity, comp_vectors, targ_vectors, comp_values, targ_values):
    cbits, tbits = nc.bit_length() - 1, nt.bit_length() - 2
    c_orders = (list(range(cbits)), list(reversed(range(cbits))))
    t_orders = (list(range(1, tbits + 1)), list(reversed(range(1, tbits + 1))))
    iblock, jblock = comp_vectors.shape[1] // nc, targ_vectors.shape[1] // nt
    chunks = 2 if jblock % 256 == 0 else 1
    width = jblock // chunks
    at_c, at_t = lax.axis_index("cmp"), lax.axis_index("tgt")

    def offset(position, order):
        return sum(((position >> (len(order) - 1 - t)) & 1) << bit for t, bit in enumerate(order))

    def table(orders, n, flip):
        mine, theirs = (jnp.array([offset(p, orders[c]) for p in range(n)], jnp.int32) for c in (flip, 1 - flip))
        return jnp.where(at_t % 2 == 0, mine, theirs)

    c_blocks = table(c_orders, nc, 0) ^ at_c
    keep = table(t_orders, nt // 2, 0) ^ at_t
    give = table(t_orders, nt // 2, 1) ^ at_t ^ 1

    def swap_c(x, t):
        pairs = [(c * nt + i, (c ^ (1 << c_orders[i % 2][t])) * nt + i) for c in range(nc) for i in range(nt)]
        return lax.ppermute(x, ("cmp", "tgt"), pairs)

    def swap_t(x, t):
        return lax.ppermute(x, "tgt", [(i, i ^ (1 << t_orders[i % 2][t])) for i in range(nt)])

    def swap_core(x):
        return lax.ppermute(x, "tgt", [(i, i ^ 1) for i in range(nt)])

    bound = 6 * 0.0625 * 0.0546875 * affinity.shape[0] * nc * affinity.shape[1] * nt
    scale = 1.0
    while bound * scale > 65000:
        scale *= 0.5

    sent, y, kept = give_product(affinity, targ_vectors, give, keep, chunks, jblock, width)
    came = [swap_core(x) for x in sent]
    mine, vc = keep_product(y, kept, comp_vectors, c_blocks, iblock)
    nears, fars = [], []
    for k in range(chunks):
        half, far = far_product(mine[k], came[k], vc, scale)
        fars.append(swap_c(far.astype(F16), 0))
        nears.append(half)
    for k in range(chunks):
        half = nears[k]
        if k > 0:
            half, fars[k - 1] = lax.optimization_barrier((half, fars[k - 1]))
        nears[k] = near_product(half, vc, scale)
    scaled = []
    for k in range(chunks):
        total = nears[k] + fars[k].astype(F32)
        for t in range(1, cbits):
            n = total.shape[1] // 2
            total = total[:, :n] + swap_c(total[:, n:].astype(F16), t).astype(F32)
        for t in range(tbits):
            n = total.shape[0] // 2
            total = total[:n] + swap_t(total[n:].astype(F16), t).astype(F32)
        lt = targ_values[k * width : (k + 1) * width]
        scaled.append((total * (1 / scale) / (lt[:, None] * comp_values[None, :] + 0.25)).astype(BF16))
    out = None
    for k in range(chunks):
        part = scaled[k]
        for t in reversed(range(tbits)):
            part = jnp.concatenate([part, swap_t(part, t)], axis=0)
        for t in reversed(range(1, cbits)):
            part = jnp.concatenate([part, swap_c(part, t)], axis=1)
        both = jnp.concatenate([keep, give])
        own, cols = mapped_product(vc, part, swap_c(part, 0), targ_vectors, both, k, jblock, width)
        out = last_product(own, swap_core(own), cols, out, k == chunks - 1)
    return out


def solution(mesh):
    in_specs = (P("cmp", "tgt"), P("cmp", None), P("tgt", None), P("cmp"), P("tgt"))
    out_specs = P("cmp", "tgt")
    body = functools.partial(shards, mesh.shape["cmp"], mesh.shape["tgt"])
    return jax.shard_map(body, mesh=mesh, in_specs=in_specs, out_specs=out_specs, check_vma=False)
```

```python
import functools

import jax
import jax.numpy as jnp
from jax import lax
from jax.experimental import pallas as pl
from jax.experimental.pallas import tpu as pltpu
from jax.sharding import PartitionSpec as P

F32, BF16, F16 = jnp.float32, jnp.bfloat16, jnp.float16
LIMIT = 10 * 1024 * 1024
TILE = 512
ORDER = [(0, 1), (1, 0), (0, 2), (0, 3), (1, 1), (0, 4), (1, 2), (0, 5), (1, 3), (1, 4), (0, 6), (1, 5), (1, 6)]
IN_VMEM = pl.BlockSpec(memory_space=pltpu.VMEM)
IN_SMEM = pl.BlockSpec(memory_space=pltpu.SMEM)
IN_HBM = pl.BlockSpec(memory_space=pltpu.HBM)


def stay(x):
    return pltpu.with_memory_space_constraint(x, pltpu.VMEM)


def leave(x):
    return pltpu.with_memory_space_constraint(x, pltpu.HBM)


def dot_nn(a, b):
    return jnp.dot(a, b, preferred_element_type=F32)


def dot_nt(a, b):
    return lax.dot_general(a, b, (((1,), (1,)), ((), ())), preferred_element_type=F32)


def tiles(n):
    return [slice(i, min(i + TILE, n)) for i in range(0, n, TILE)]


def call(kernel, name, in_specs, args, out_specs, out_shape, scratch, flops, aliases=None):
    return pl.pallas_call(
        kernel,
        name=name,
        in_specs=in_specs,
        out_specs=out_specs,
        out_shape=out_shape,
        scratch_shapes=scratch,
        input_output_aliases=aliases or {},
        cost_estimate=pl.CostEstimate(flops=flops // 100, bytes_accessed=0, transcendentals=0),
        compiler_params=pltpu.CompilerParams(vmem_limit_bytes=LIMIT),
    )(*args)


def column_copies(idx, source, target, block, start, width, sem):
    found = []
    for q in range(target.shape[1] // width):
        at = pl.multiple_of(idx[q] * block + start, width)
        found.append(pltpu.make_async_copy(source.at[:, pl.ds(at, width)], target.at[:, pl.ds(q * width, width)], sem.at[q]))
    return found


def half_product(y, cols, aff, fetch, dtype):
    rows, depth = aff.shape
    spans = tiles(rows)
    wide = (fetch[0][5].stop - fetch[0][5].start) * fetch[0][4] if cols is None else cols.shape[1]
    sources = []
    for f in fetch:
        if not any(f[0] is x for x in sources):
            sources.append(f[0])
    tables = []
    for f in fetch:
        if not any(f[1] is x for x in tables):
            tables.append(f[1])

    def place(x, among):
        return [i for i, z in enumerate(among) if z is x][0]

    def kernel(*refs):
        refs = list(refs)
        idx = [refs.pop(0) for _ in tables]
        from_hbm = [refs.pop(0) for _ in sources]
        a = refs.pop(0)
        c = refs.pop(0) if cols is not None else None
        out = refs.pop(0)
        loads = []
        if y is None:
            source, a = a, refs.pop(0)
        got = [refs.pop(0) for _ in fetch]
        if y is None:
            y_sem = refs.pop(0)
            loads = [pltpu.make_async_copy(source.at[s, :], a.at[s, :], y_sem.at[i]) for i, s in enumerate(spans)]
        moves = []
        for f, to in zip(fetch, got):
            sem = refs.pop(0)
            group = []
            for i, q in enumerate(range(f[5].start, f[5].stop)):
                at = pl.multiple_of(idx[place(f[1], tables)][q] * f[2] + f[3], f[4])
                part = from_hbm[place(f[0], sources)].at[:, pl.ds(at, f[4])]
                group.append(pltpu.make_async_copy(part, to.at[:, pl.ds(i * f[4], f[4])], sem.at[i]))
            moves.append(group)
        queue = [[load] for load in loads]
        if cols is None:
            queue[0] = moves[0] + queue[0]
            queue += moves[1:]
        else:
            queue += moves
        begun = 0
        for group in queue[:2]:
            begun += 1
            for move in group:
                move.start()
        if cols is None:
            for move in moves[0]:
                move.wait()
            c = got[0]
        for i, s in enumerate(spans):
            if loads:
                loads[i].wait()
            if begun < len(queue):
                for move in queue[begun]:
                    move.start()
                begun += 1
            out[:, s] = dot_nn(a[s, :], c[...]).astype(dtype).T
        for group in queue[begun:]:
            for move in group:
                move.start()
        for group in moves[1:] if cols is None else moves:
            for move in group:
                move.wait()

    out_shape = [pltpu.VMEM((wide, rows), dtype)]
    args = tables + [leave(x) for x in sources]
    in_specs = [IN_SMEM] * len(tables) + [IN_HBM] * len(sources)
    scratch = []
    if y is None:
        args.append(leave(aff))
        in_specs.append(IN_HBM)
        out_shape.append(pltpu.VMEM(aff.shape, BF16))
        scratch.append(pltpu.SemaphoreType.DMA((len(spans),)))
    else:
        args.append(stay(y))
        in_specs.append(IN_VMEM)
    if cols is not None:
        args.append(stay(cols))
        in_specs.append(IN_VMEM)
    for f in fetch:
        n = f[5].stop - f[5].start
        out_shape.append(pltpu.VMEM((f[0].shape[0], n * f[4]), BF16))
        scratch.append(pltpu.SemaphoreType.DMA((n,)))
    return call(
        kernel, "half", in_specs, args, [IN_VMEM] * len(out_shape), out_shape, scratch, 2 * rows * depth * wide
    )


def far_product(mine, came, vc, scale):
    wide, rows = mine.shape

    def kernel(h, r, w, half, out):
        half[...] = (h[...] + r[...].astype(F32)).astype(BF16)
        for t in tiles(vc.shape[1]):
            out[:, t] = dot_nn(half[...], w[:, t]) * scale

    out_shape = [pltpu.VMEM((wide, rows), BF16), jax.ShapeDtypeStruct((wide, vc.shape[1]), F32)]
    return call(
        kernel, "far", [IN_VMEM] * 3, [stay(mine), stay(came), stay(vc)], [IN_VMEM] * 2, out_shape, [],
        2 * wide * rows * vc.shape[1],
    )


def near_product(half, vc, scale, vt, idx, k, block, width):
    wide, rows = half.shape
    n, depth = idx.shape[0], vt.shape[0]

    def kernel(s, h, w, v, out, cols, sem):
        moves = column_copies(s, v, cols, block, k * width, width, sem)
        for move in moves:
            move.start()
        for t in tiles(vc.shape[1]):
            out[:, t] = dot_nn(h[...], w[:, t]) * scale
        for move in moves:
            move.wait()

    out_shape = [jax.ShapeDtypeStruct((wide, vc.shape[1]), F32), pltpu.VMEM((depth, 2 * wide), BF16)]
    return call(
        kernel, "near", [IN_SMEM] + [IN_VMEM] * 2 + [IN_HBM], [idx, stay(half), stay(vc), leave(vt)], [IN_VMEM] * 2,
        out_shape, [pltpu.SemaphoreType.DMA((n,))], 2 * wide * rows * vc.shape[1],
    )


def mapped_product(vc_near, vc_far, near, far, part):
    rows, wide = part.stop - part.start, near.shape[0]

    def kernel(v, w, a, b, out):
        for t in tiles(rows):
            at = slice(part.start + t.start, part.start + t.stop)
            out[t, :] = (dot_nt(v[at, :], a[...]) + dot_nt(w[at, :], b[...])).astype(BF16)

    return call(
        kernel, "mapped", [IN_VMEM] * 4, [stay(vc_near), stay(vc_far), stay(near), stay(far)], IN_VMEM,
        jax.ShapeDtypeStruct((rows, wide), BF16), [], 4 * rows * vc_near.shape[1] * wide,
    )


def middle_product(own, other, cols, before):
    rows, wide = own.shape

    def kernel(m, r, c, *refs):
        for s in [slice(i, i + 256) for i in range(0, rows, 256)]:
            value = dot_nt(m[s, :], c[:, :wide]) + dot_nt(r[s, :], c[:, wide:])
            refs[-1][s, :] = value if before is None else value + refs[0][s, :]

    args = [stay(own), stay(other), stay(cols)] + ([] if before is None else [stay(before)])
    return call(
        kernel, "predicted", [IN_VMEM] * len(args), args, IN_VMEM, pltpu.VMEM((rows, cols.shape[0]), F32), [],
        4 * rows * cols.shape[0] * wide,
    )


def last_product(own, other, cols, before, out, part, rows):
    wide, depth = own.shape[1], cols.shape[0]
    spans = [slice(i, i + 256) for i in range(0, part.stop - part.start, 256)]
    slots = 4

    def kernel(m, r, c, *refs):
        to, held, sem = refs[-3:]
        moves = []
        for i, s in enumerate(spans):
            at = slice(part.start + s.start, part.start + s.stop)
            if i >= slots:
                moves[i - slots].wait()
            value = dot_nt(m[s, :], c[:, :wide]) + dot_nt(r[s, :], c[:, wide:])
            held[i % slots] = value if before is None else value + refs[0][at, :]
            moves.append(pltpu.make_async_copy(held.at[i % slots], to.at[at, :], sem.at[i % slots]))
            moves[i].start()
        for move in moves[-slots:]:
            move.wait()

    args = [stay(own), stay(other), stay(cols)] + ([] if before is None else [stay(before)])
    in_specs = [IN_VMEM] * len(args)
    aliases = {}
    if out is not None:
        aliases = {len(args): 0}
        args.append(leave(out))
        in_specs.append(IN_HBM)
    scratch = [pltpu.VMEM((slots, 256, depth), F32), pltpu.SemaphoreType.DMA((slots,))]
    return call(
        kernel, "predicted", in_specs, args, IN_HBM, jax.ShapeDtypeStruct((rows, depth), F32), scratch,
        4 * (part.stop - part.start) * depth * wide, aliases,
    )


def shards(nc, nt, affinity, comp_vectors, targ_vectors, comp_values, targ_values):
    cbits, tbits = nc.bit_length() - 1, nt.bit_length() - 2
    c_orders = (list(range(cbits)), list(reversed(range(cbits))))
    t_orders = (list(range(1, tbits + 1)), list(reversed(range(1, tbits + 1))))
    iblock, jblock = comp_vectors.shape[1] // nc, targ_vectors.shape[1] // nt
    chunks = 2 if jblock % 256 == 0 else 1
    width = jblock // chunks
    at_c, at_t = lax.axis_index("cmp"), lax.axis_index("tgt")

    def offset(position, order):
        return sum(((position >> (len(order) - 1 - t)) & 1) << bit for t, bit in enumerate(order))

    def table(orders, n, flip):
        mine, theirs = (jnp.array([offset(p, orders[c]) for p in range(n)], jnp.int32) for c in (flip, 1 - flip))
        return jnp.where(at_t % 2 == 0, mine, theirs)

    c_blocks = table(c_orders, nc, 0) ^ at_c
    keep = table(t_orders, nt // 2, 0) ^ at_t
    give = table(t_orders, nt // 2, 1) ^ at_t ^ 1

    def swap_c(x, t):
        pairs = [(c * nt + i, (c ^ (1 << c_orders[i % 2][t])) * nt + i) for c in range(nc) for i in range(nt)]
        return lax.ppermute(x, ("cmp", "tgt"), pairs)

    def swap_t(x, t):
        return lax.ppermute(x, "tgt", [(i, i ^ (1 << t_orders[i % 2][t])) for i in range(nt)])

    def swap_core(x):
        return lax.ppermute(x, "tgt", [(i, i ^ 1) for i in range(nt)])

    bound = 6 * 0.0625 * 0.0546875 * affinity.shape[0] * nc * affinity.shape[1] * nt
    scale = 1.0
    while bound * scale > 65000:
        scale *= 0.5

    kinds = "c" * cbits + "t" * tbits
    steps = [(kind, kinds[:i].count(kind)) for i, kind in enumerate(kinds)]
    count = len(steps)

    def exchange(x, i):
        kind, t = steps[i]
        return swap_c(x, t) if kind == "c" else swap_t(x, t)

    def after(x, y):
        return lax.optimization_barrier((x, y))[0]

    every, upper, lower = slice(0, nt // 2), slice(nc // 2, nc), slice(0, nc // 2)
    give_cols = [(targ_vectors, give, jblock, k * width, width, every) for k in range(chunks)]
    keep_cols = [(targ_vectors, keep, jblock, k * width, width, every) for k in range(chunks)]
    vc_cols = [(comp_vectors, c_blocks, iblock, 0, iblock, part) for part in (upper, lower)]
    both = jnp.concatenate([keep, give])
    if chunks == 2:
        sent, y, _, given = half_product(None, None, affinity, give_cols, BF16)
        came = [swap_core(sent)]
        sent, *kept, vc_far = half_product(y, given, affinity, keep_cols + vc_cols[:1], BF16)
        came.append(swap_core(sent))
    else:
        sent, y, _, *kept, vc_far = half_product(None, None, affinity, give_cols + keep_cols + vc_cols[:1], BF16)
        came = [swap_core(sent)]
    mine, vc_near = half_product(y, kept[0], affinity, vc_cols[1:], F32)
    half, far = far_product(mine, came[0], vc_far, scale)
    coming = [exchange(far.astype(F16), 0)]
    near, cols = near_product(half, vc_near, scale, targ_vectors, both, 0, jblock, width)
    nears, columns = [near], [cols]
    token = near
    if chunks == 2:
        mine = half_product(after(y, near), kept[1], affinity, [], F32)[0]
        half, far = far_product(mine, came[1], vc_far, scale)
        token = far
    held = list(nears)
    rows = affinity.shape[0]
    total = out = None

    def event(k, i, token):
        came = after(coming[k], token)
        if i < count:
            total = held[k] + came.astype(F32)
            if i < count - 1:
                n = total.shape[steps[i + 1][0] == "c"] // 2
                held[k], goes = (total[:, :n], total[:, n:]) if steps[i + 1][0] == "c" else (total[:n], total[n:])
                goes = goes.astype(F16)
                coming[k] = exchange(goes, i + 1)
                return goes
            lt = targ_values[k * width : (k + 1) * width]
            held[k] = (total * (1 / scale) / (lt[:, None] * comp_values[None, :] + 0.25)).astype(BF16)
        else:
            held[k] = jnp.concatenate([held[k], came], axis=int(steps[2 * count - 1 - i][0] == "c"))
        coming[k] = exchange(held[k], 2 * count - 2 - i)
        return held[k]

    token = event(0, 0, token)
    if chunks == 2:
        goes = after(far, token).astype(F16)
        coming.append(exchange(goes, 0))
        near, cols = near_product(after(half, goes), vc_near, scale, targ_vectors, both, 1, jblock, width)
        held.append(near)
        columns.append(cols)
    order = [(0, i) for i in range(1, 2 * count - 1)]
    if chunks == 2:
        late = [(1, i) for i in range(2 * count - 1)]
        order = ORDER if count == 4 else [x for pair in zip(order + [None], late) for x in pair if x]
    for k, i in order:
        token = event(k, i, token)
    for k in range(chunks):
        spans = [slice(0, rows)] if k < chunks - 1 else [slice(0, rows // 2), slice(rows // 2, rows)]
        last = after(coming[k], token)
        own = [mapped_product(vc_near, vc_far, held[k], last, s) for s in spans]
        other = [swap_core(x) for x in own]
        if k < chunks - 1:
            total = token = middle_product(own[0], other[0], columns[k], total)
        else:
            for m, r, s in zip(own, other, spans):
                out = last_product(m, r, columns[k], total, out, s, rows)
    return out


def solution(mesh):
    in_specs = (P("cmp", "tgt"), P("cmp", None), P("tgt", None), P("cmp"), P("tgt"))
    out_specs = P("cmp", "tgt")
    body = functools.partial(shards, mesh.shape["cmp"], mesh.shape["tgt"])
    return jax.shard_map(body, mesh=mesh, in_specs=in_specs, out_specs=out_specs, check_vma=False)
```

```python
import functools

import jax
import jax.numpy as jnp
from jax import lax
from jax.experimental import pallas as pl
from jax.experimental.pallas import tpu as pltpu
from jax.sharding import PartitionSpec as P

F32, BF16, F16 = jnp.float32, jnp.bfloat16, jnp.float16
LIMIT = 10 * 1024 * 1024
TILE = 512
ORDER = [(0, 2), (1, 0), (0, 3), (1, 1), (0, 4), (1, 2), (0, 5), (1, 3), (1, 4), (0, 6), (1, 5), (1, 6)]
IN_VMEM = pl.BlockSpec(memory_space=pltpu.VMEM)
IN_HBM = pl.BlockSpec(memory_space=pltpu.HBM)


def stay(x):
    return pltpu.with_memory_space_constraint(x, pltpu.VMEM)


def leave(x):
    return pltpu.with_memory_space_constraint(x, pltpu.HBM)


def dot_nn(a, b):
    return jnp.dot(a, b, preferred_element_type=F32)


def dot_nt(a, b):
    return lax.dot_general(a, b, (((1,), (1,)), ((), ())), preferred_element_type=F32)


def tiles(n):
    return [slice(i, min(i + TILE, n)) for i in range(0, n, TILE)]


def call(kernel, name, in_specs, args, out_specs, out_shape, scratch, flops, aliases=None):
    return pl.pallas_call(
        kernel,
        name=name,
        in_specs=in_specs,
        out_specs=out_specs,
        out_shape=out_shape,
        scratch_shapes=scratch,
        input_output_aliases=aliases or {},
        cost_estimate=pl.CostEstimate(flops=flops // 100, bytes_accessed=0, transcendentals=0),
        compiler_params=pltpu.CompilerParams(vmem_limit_bytes=LIMIT),
    )(*args)


def column_copies(idx, source, target, block, start, width, sem):
    found = []
    for q in range(target.shape[1] // width):
        at = pl.multiple_of(idx(q) * block + start, width)
        found.append(pltpu.make_async_copy(source.at[:, pl.ds(at, width)], target.at[:, pl.ds(q * width, width)], sem.at[q]))
    return found


def half_product(y, cols, aff, fetch, dtype):
    rows, depth = aff.shape
    spans = tiles(rows)
    wide = (fetch[0][5].stop - fetch[0][5].start) * fetch[0][4] if cols is None else cols.shape[1]
    sources = []
    for f in fetch:
        if not any(f[0] is x for x in sources):
            sources.append(f[0])
    def place(x, among):
        return [i for i, z in enumerate(among) if z is x][0]

    def kernel(*refs):
        refs = list(refs)
        from_hbm = [refs.pop(0) for _ in sources]
        a = refs.pop(0)
        c = refs.pop(0) if cols is not None else None
        out = refs.pop(0)
        loads = []
        if y is None:
            source, a = a, refs.pop(0)
        got = [refs.pop(0) for _ in fetch]
        if y is None:
            y_sem = refs.pop(0)
            loads = [pltpu.make_async_copy(source.at[s, :], a.at[s, :], y_sem.at[i]) for i, s in enumerate(spans)]
        moves = []
        for f, to in zip(fetch, got):
            sem = refs.pop(0)
            group = []
            step = min(128, f[4])
            for i, q in enumerate(range(f[5].start, f[5].stop)):
                for j in range(0, f[4], step):
                    at = pl.multiple_of(f[1](q) * f[2] + f[3] + j, step)
                    part = from_hbm[place(f[0], sources)].at[:, pl.ds(at, step)]
                    here = i * f[4] + j
                    group.append(pltpu.make_async_copy(part, to.at[:, pl.ds(here, step)], sem.at[here // step]))
            moves.append(group)
        queue = [[load] for load in loads]
        if cols is None:
            queue[0] = moves[0] + queue[0]
            queue += moves[1:]
        else:
            queue += moves
        begun = 0
        for group in queue[: 2 if loads else len(queue)]:
            begun += 1
            for move in group:
                move.start()
        if cols is None:
            for move in moves[0]:
                move.wait()
            c = got[0]
        for i, s in enumerate(spans):
            if loads:
                loads[i].wait()
            if begun < len(queue):
                for move in queue[begun]:
                    move.start()
                begun += 1
            out[:, s] = dot_nn(a[s, :], c[...]).astype(dtype).T
        for group in queue[begun:]:
            for move in group:
                move.start()
        for group in moves[1:] if cols is None else moves:
            for move in group:
                move.wait()

    out_shape = [pltpu.VMEM((wide, rows), dtype)]
    args = [leave(x) for x in sources]
    in_specs = [IN_HBM] * len(sources)
    scratch = []
    if y is None:
        args.append(leave(aff))
        in_specs.append(IN_HBM)
        out_shape.append(pltpu.VMEM(aff.shape, BF16))
        scratch.append(pltpu.SemaphoreType.DMA((len(spans),)))
    else:
        args.append(stay(y))
        in_specs.append(IN_VMEM)
    if cols is not None:
        args.append(stay(cols))
        in_specs.append(IN_VMEM)
    for f in fetch:
        n = f[5].stop - f[5].start
        out_shape.append(pltpu.VMEM((f[0].shape[0], n * f[4]), BF16))
        scratch.append(pltpu.SemaphoreType.DMA((n * f[4] // min(128, f[4]),)))
    return call(
        kernel, "half", in_specs, args, [IN_VMEM] * len(out_shape), out_shape, scratch, 2 * rows * depth * wide
    )


def far_product(mine, came, vc, scale):
    wide, rows = mine.shape

    def kernel(h, r, w, half, out):
        half[...] = (h[...] + r[...].astype(F32)).astype(BF16)
        for t in tiles(vc.shape[1]):
            out[:, t] = dot_nn(half[...], w[:, t]) * scale

    out_shape = [pltpu.VMEM((wide, rows), BF16), jax.ShapeDtypeStruct((wide, vc.shape[1]), F32)]
    return call(
        kernel, "far", [IN_VMEM] * 3, [stay(mine), stay(came), stay(vc)], [IN_VMEM] * 2, out_shape, [],
        2 * wide * rows * vc.shape[1],
    )


def near_product(half, vc, scale, vt, idx, n, wanted, block, width):
    wide, rows = half.shape
    depth = vt.shape[0]

    def kernel(h, w, v, out, *refs):
        moves = []
        for k, cols, sem in zip(wanted, refs, refs[len(wanted) :]):
            moves += column_copies(idx, v, cols, block, k * width, width, sem)
        for move in moves:
            move.start()
        for t in tiles(vc.shape[1]):
            out[:, t] = dot_nn(h[...], w[:, t]) * scale
        for move in moves:
            move.wait()

    out_shape = [jax.ShapeDtypeStruct((wide, vc.shape[1]), F32)] + [pltpu.VMEM((depth, 2 * wide), BF16)] * len(wanted)
    near, *cols = call(
        kernel, "near", [IN_VMEM] * 2 + [IN_HBM], [stay(half), stay(vc), leave(vt)],
        [IN_VMEM] * len(out_shape), out_shape, [pltpu.SemaphoreType.DMA((n,))] * len(wanted), 2 * wide * rows * vc.shape[1],
    )
    return near, cols


def mapped_product(vc_near, vc_far, near, far, part):
    rows, wide = part.stop - part.start, near.shape[0]

    def kernel(v, w, a, b, out):
        for t in tiles(rows):
            at = slice(part.start + t.start, part.start + t.stop)
            out[t, :] = (dot_nt(v[at, :], a[...]) + dot_nt(w[at, :], b[...])).astype(BF16)

    return call(
        kernel, "mapped", [IN_VMEM] * 4, [stay(vc_near), stay(vc_far), stay(near), stay(far)], IN_VMEM,
        jax.ShapeDtypeStruct((rows, wide), BF16), [], 4 * rows * vc_near.shape[1] * wide,
    )


def middle_product(own, other, cols, before):
    rows, wide = own.shape

    def kernel(m, r, c, *refs):
        for s in [slice(i, i + 256) for i in range(0, rows, 256)]:
            value = dot_nt(m[s, :], c[:, :wide]) + dot_nt(r[s, :], c[:, wide:])
            refs[-1][s, :] = value if before is None else value + refs[0][s, :]

    args = [stay(own), stay(other), stay(cols)] + ([] if before is None else [stay(before)])
    return call(
        kernel, "predicted", [IN_VMEM] * len(args), args, IN_VMEM, pltpu.VMEM((rows, cols.shape[0]), F32), [],
        4 * rows * cols.shape[0] * wide,
    )


def last_product(own, other, cols, before, out, part, rows):
    wide, depth = own.shape[1], cols.shape[0]
    spans = [slice(i, i + 256) for i in range(0, part.stop - part.start, 256)]
    slots = 4

    def kernel(m, r, c, *refs):
        to, held, sem = refs[-3:]
        moves = []
        for i, s in enumerate(spans):
            at = slice(part.start + s.start, part.start + s.stop)
            if i >= slots:
                moves[i - slots].wait()
            value = dot_nt(m[s, :], c[:, :wide]) + dot_nt(r[s, :], c[:, wide:])
            held[i % slots] = value if before is None else value + refs[0][at, :]
            moves.append(pltpu.make_async_copy(held.at[i % slots], to.at[at, :], sem.at[i % slots]))
            moves[i].start()
        for move in moves[-slots:]:
            move.wait()

    args = [stay(own), stay(other), stay(cols)] + ([] if before is None else [stay(before)])
    in_specs = [IN_VMEM] * len(args)
    aliases = {}
    if out is not None:
        aliases = {len(args): 0}
        args.append(leave(out))
        in_specs.append(IN_HBM)
    scratch = [pltpu.VMEM((slots, 256, depth), F32), pltpu.SemaphoreType.DMA((slots,))]
    return call(
        kernel, "predicted", in_specs, args, IN_HBM, jax.ShapeDtypeStruct((rows, depth), F32), scratch,
        4 * (part.stop - part.start) * depth * wide, aliases,
    )


def shards(nc, nt, affinity, comp_vectors, targ_vectors, comp_values, targ_values):
    cbits, tbits = nc.bit_length() - 1, nt.bit_length() - 2
    c_orders = (list(range(cbits)), list(reversed(range(cbits))))
    t_orders = (list(range(1, tbits + 1)), list(reversed(range(1, tbits + 1))))
    iblock, jblock = comp_vectors.shape[1] // nc, targ_vectors.shape[1] // nt
    chunks = 2 if jblock % 256 == 0 else 1
    width = jblock // chunks

    def offset(position, order):
        return sum(((position >> (len(order) - 1 - t)) & 1) << bit for t, bit in enumerate(order))

    def pick(orders, position, flip, core):
        return jnp.where(core == 0, offset(position, orders[flip]), offset(position, orders[1 - flip]))

    def c_blocks(p):
        return lax.axis_index("cmp") ^ pick(c_orders, p, 0, lax.axis_index("tgt") % 2)

    def keep(q):
        at = lax.axis_index("tgt")
        return at ^ pick(t_orders, q, 0, at % 2)

    def give(q):
        at = lax.axis_index("tgt")
        return at ^ 1 ^ pick(t_orders, q, 1, at % 2)

    def both(q):
        return keep(q) if q < nt // 2 else give(q - nt // 2)

    def swap_c(x, t):
        pairs = [(c * nt + i, (c ^ (1 << c_orders[i % 2][t])) * nt + i) for c in range(nc) for i in range(nt)]
        return lax.ppermute(x, ("cmp", "tgt"), pairs)

    def swap_t(x, t):
        return lax.ppermute(x, "tgt", [(i, i ^ (1 << t_orders[i % 2][t])) for i in range(nt)])

    def swap_core(x):
        return lax.ppermute(x, "tgt", [(i, i ^ 1) for i in range(nt)])

    bound = 6 * 0.0625 * 0.0546875 * affinity.shape[0] * nc * affinity.shape[1] * nt
    scale = 1.0
    while bound * scale > 65000:
        scale *= 0.5

    kinds = "c" * cbits + "t" * tbits
    steps = [(kind, kinds[:i].count(kind)) for i, kind in enumerate(kinds)]
    count = len(steps)

    def exchange(x, i):
        kind, t = steps[i]
        return swap_c(x, t) if kind == "c" else swap_t(x, t)

    def after(x, y):
        return lax.optimization_barrier((x, y))[0]

    every, upper, lower = slice(0, nt // 2), slice(nc // 2, nc), slice(0, nc // 2)
    give_cols = [(targ_vectors, give, jblock, k * width, width, every) for k in range(chunks)]
    keep_cols = [(targ_vectors, keep, jblock, k * width, width, every) for k in range(chunks)]
    vc_cols = [(comp_vectors, c_blocks, iblock, 0, iblock, part) for part in (upper, lower)]
    if chunks == 2:
        sent, y, _, given = half_product(None, None, affinity, give_cols, BF16)
        came = [swap_core(sent)]
        sent, *kept = half_product(y, given, affinity, keep_cols, BF16)
        came.append(swap_core(sent))
        mine, vc_far = half_product(y, kept[0], affinity, vc_cols[:1], F32)
    else:
        sent, y, _, *kept = half_product(None, None, affinity, give_cols + keep_cols, BF16)
        came = [swap_core(sent)]
        mine, vc_far, vc_near = half_product(y, kept[0], affinity, vc_cols, F32)
    pair_values = swap_t(targ_values, tbits - 1)
    half, far = far_product(mine, came[0], vc_far, scale)
    coming = [exchange(far.astype(F16), 0)]
    token = far
    if chunks == 2:
        mine, vc_near = half_product(after(y, far), kept[1], affinity, vc_cols[1:], F32)
        late_half, late_far = far_product(mine, came[1], vc_far, scale)
        token = late_far
    near, columns = near_product(
        after(half, token), vc_near, scale, targ_vectors, both, nt, [] if chunks == 2 else [0], jblock, width
    )
    token, nears = near, [near]
    held = list(nears)
    rows = affinity.shape[0]
    total = out = None

    def event(k, i, token):
        came = after(coming[k], token)
        if i == count - 1:
            n = came.shape[0] // 2
            came = jnp.concatenate([came[n:], came[:n]])
        if i < count:
            total = held[k] + came.astype(F32)
            if i < count - 2:
                n = total.shape[steps[i + 1][0] == "c"] // 2
                held[k], goes = (total[:, :n], total[:, n:]) if steps[i + 1][0] == "c" else (total[:n], total[n:])
            else:
                held[k] = goes = total
            if i < count - 1:
                goes = goes.astype(F16)
                coming[k] = exchange(goes, i + 1)
                return goes
            lt = jnp.concatenate([x[k * width : (k + 1) * width] for x in (targ_values, pair_values)])
            held[k] = (total * (1 / scale) / (lt[:, None] * comp_values[None, :] + 0.25)).astype(BF16)
        else:
            held[k] = jnp.concatenate([held[k], came], axis=int(steps[2 * count - 2 - i][0] == "c"))
        coming[k] = exchange(held[k], 2 * count - 3 - i)
        return held[k]

    final = 2 * count - 2
    token = event(0, 0, token)
    if chunks == 2:
        token = event(0, 1, token)
        goes = after(late_far, token).astype(F16)
        coming.append(exchange(goes, 0))
        near, columns = near_product(after(late_half, goes), vc_near, scale, targ_vectors, both, nt, [0, 1], jblock, width)
        held.append(near)
    order = [(0, i) for i in range(chunks, final + 1)]
    if chunks == 2:
        late = [(1, i) for i in range(final + 1)]
        order = ORDER if count == 4 else [x for pair in zip(order + [None], late) for x in pair if x]
    whole, parts = [slice(0, rows)], [slice(0, rows // 2), slice(rows // 2, rows)]
    for k, i in order:
        if i < final:
            token = event(k, i, token)
            if (k, i) == (chunks - 1, final - 1) and chunks > 1:
                early, _ = lax.optimization_barrier((early, token))
                total = token = middle_product(early, swap_core(early), columns[0], None)
        else:
            last = after(coming[k], token)
            mapped = [mapped_product(vc_near, vc_far, held[k], last, s) for s in (whole if k < chunks - 1 else parts)]
            early = token = mapped[0]
    for x, s in zip(mapped, parts):
        out = last_product(x, swap_core(x), columns[chunks - 1], total, out, s, rows)
    return out


def solution(mesh):
    in_specs = (P("cmp", "tgt"), P("cmp", None), P("tgt", None), P("cmp"), P("tgt"))
    out_specs = P("cmp", "tgt")
    body = functools.partial(shards, mesh.shape["cmp"], mesh.shape["tgt"])
    return jax.shard_map(body, mesh=mesh, in_specs=in_specs, out_specs=out_specs, check_vma=False)
```

```python
import functools

import jax
import jax.numpy as jnp
from jax import lax
from jax.experimental import pallas as pl
from jax.experimental.pallas import tpu as pltpu
from jax.sharding import PartitionSpec as P

F32, BF16, F16 = jnp.float32, jnp.bfloat16, jnp.float16
LIMIT = 10 * 1024 * 1024
TILE = 512
ORDER = [(0, 2), (1, 0), (0, 3), (1, 1), (0, 4), (1, 2), (0, 5), (1, 3), (1, 4), (0, 6), (1, 5), (1, 6)]
IN_VMEM = pl.BlockSpec(memory_space=pltpu.VMEM)
IN_HBM = pl.BlockSpec(memory_space=pltpu.HBM)


def stay(x):
    return pltpu.with_memory_space_constraint(x, pltpu.VMEM)


def leave(x):
    return pltpu.with_memory_space_constraint(x, pltpu.HBM)


def dot_nn(a, b):
    return jnp.dot(a, b, preferred_element_type=F32)


def dot_nt(a, b):
    return lax.dot_general(a, b, (((1,), (1,)), ((), ())), preferred_element_type=F32)


def tiles(n):
    return [slice(i, min(i + TILE, n)) for i in range(0, n, TILE)]


def call(kernel, name, in_specs, args, out_specs, out_shape, scratch, flops, aliases=None):
    return pl.pallas_call(
        kernel,
        name=name,
        in_specs=in_specs,
        out_specs=out_specs,
        out_shape=out_shape,
        scratch_shapes=scratch,
        input_output_aliases=aliases or {},
        cost_estimate=pl.CostEstimate(flops=flops // 100, bytes_accessed=0, transcendentals=0),
        compiler_params=pltpu.CompilerParams(vmem_limit_bytes=LIMIT),
    )(*args)


def column_copies(idx, source, target, block, start, width, sem):
    found = []
    for q in range(target.shape[1] // width):
        at = pl.multiple_of(idx(q) * block + start, width)
        found.append(pltpu.make_async_copy(source.at[:, pl.ds(at, width)], target.at[:, pl.ds(q * width, width)], sem.at[q]))
    return found


def half_product(y, cols, aff, fetch, dtype):
    rows, depth = aff.shape
    spans = tiles(rows)
    wide = (fetch[0][5].stop - fetch[0][5].start) * fetch[0][4] if cols is None else cols.shape[1]
    sources = []
    for f in fetch:
        if not any(f[0] is x for x in sources):
            sources.append(f[0])
    def place(x, among):
        return [i for i, z in enumerate(among) if z is x][0]

    def kernel(*refs):
        refs = list(refs)
        from_hbm = [refs.pop(0) for _ in sources]
        a = refs.pop(0)
        c = refs.pop(0) if cols is not None else None
        out = refs.pop(0)
        loads = []
        if y is None:
            source, a = a, refs.pop(0)
        got = [refs.pop(0) for _ in fetch]
        if y is None:
            y_sem = refs.pop(0)
            loads = [pltpu.make_async_copy(source.at[s, :], a.at[s, :], y_sem.at[i]) for i, s in enumerate(spans)]
        moves = []
        for f, to in zip(fetch, got):
            sem = refs.pop(0)
            group = []
            step = min(128, f[4])
            for i, q in enumerate(range(f[5].start, f[5].stop)):
                for j in range(0, f[4], step):
                    at = pl.multiple_of(f[1](q) * f[2] + f[3] + j, step)
                    part = from_hbm[place(f[0], sources)].at[:, pl.ds(at, step)]
                    here = i * f[4] + j
                    group.append(pltpu.make_async_copy(part, to.at[:, pl.ds(here, step)], sem.at[here // step]))
            moves.append(group)
        queue = [[load] for load in loads]
        if cols is None:
            queue[0] = moves[0] + queue[0]
            queue += moves[1:]
        else:
            queue += moves
        begun = 0
        for group in queue[: 2 if loads else len(queue)]:
            begun += 1
            for move in group:
                move.start()
        if cols is None:
            for move in moves[0]:
                move.wait()
            c = got[0]
        for i, s in enumerate(spans):
            if loads:
                loads[i].wait()
            if begun < len(queue):
                for move in queue[begun]:
                    move.start()
                begun += 1
            out[:, s] = dot_nn(a[s, :], c[...]).astype(dtype).T
        for group in queue[begun:]:
            for move in group:
                move.start()
        for group in moves[1:] if cols is None else moves:
            for move in group:
                move.wait()

    out_shape = [pltpu.VMEM((wide, rows), dtype)]
    args = [leave(x) for x in sources]
    in_specs = [IN_HBM] * len(sources)
    scratch = []
    if y is None:
        args.append(leave(aff))
        in_specs.append(IN_HBM)
        out_shape.append(pltpu.VMEM(aff.shape, BF16))
        scratch.append(pltpu.SemaphoreType.DMA((len(spans),)))
    else:
        args.append(stay(y))
        in_specs.append(IN_VMEM)
    if cols is not None:
        args.append(stay(cols))
        in_specs.append(IN_VMEM)
    for f in fetch:
        n = f[5].stop - f[5].start
        out_shape.append(pltpu.VMEM((f[0].shape[0], n * f[4]), BF16))
        scratch.append(pltpu.SemaphoreType.DMA((n * f[4] // min(128, f[4]),)))
    return call(
        kernel, "half", in_specs, args, [IN_VMEM] * len(out_shape), out_shape, scratch, 2 * rows * depth * wide
    )


def far_product(mine, came, vc, scale):
    wide, rows = mine.shape

    def kernel(h, r, w, half, out):
        half[...] = (h[...] + r[...].astype(F32)).astype(BF16)
        for t in tiles(vc.shape[1]):
            out[:, t] = dot_nn(half[...], w[:, t]) * scale

    out_shape = [pltpu.VMEM((wide, rows), BF16), jax.ShapeDtypeStruct((wide, vc.shape[1]), F32)]
    return call(
        kernel, "far", [IN_VMEM] * 3, [stay(mine), stay(came), stay(vc)], [IN_VMEM] * 2, out_shape, [],
        2 * wide * rows * vc.shape[1],
    )


def near_product(half, vc, scale, vt, idx, n, wanted, block, width):
    wide, rows = half.shape
    depth = vt.shape[0]

    def kernel(h, w, v, out, *refs):
        moves = []
        for k, cols, sem in zip(wanted, refs, refs[len(wanted) :]):
            moves += column_copies(idx, v, cols, block, k * width, width, sem)
        for move in moves:
            move.start()
        for t in tiles(vc.shape[1]):
            out[:, t] = dot_nn(h[...], w[:, t]) * scale
        for move in moves:
            move.wait()

    out_shape = [jax.ShapeDtypeStruct((wide, vc.shape[1]), F32)] + [pltpu.VMEM((depth, 2 * wide), BF16)] * len(wanted)
    near, *cols = call(
        kernel, "near", [IN_VMEM] * 2 + [IN_HBM], [stay(half), stay(vc), leave(vt)],
        [IN_VMEM] * len(out_shape), out_shape, [pltpu.SemaphoreType.DMA((n,))] * len(wanted), 2 * wide * rows * vc.shape[1],
    )
    return near, cols


def mapped_product(vc_near, vc_far, near, far, part):
    rows, wide = part.stop - part.start, near.shape[0]

    def kernel(v, w, a, b, out):
        for t in tiles(rows):
            at = slice(part.start + t.start, part.start + t.stop)
            out[t, :] = (dot_nt(v[at, :], a[...]) + dot_nt(w[at, :], b[...])).astype(BF16)

    return call(
        kernel, "mapped", [IN_VMEM] * 4, [stay(vc_near), stay(vc_far), stay(near), stay(far)], IN_VMEM,
        jax.ShapeDtypeStruct((rows, wide), BF16), [], 4 * rows * vc_near.shape[1] * wide,
    )


def middle_product(own, other, cols, before):
    rows, wide = own.shape

    def kernel(m, r, c, *refs):
        for s in [slice(i, i + 256) for i in range(0, rows, 256)]:
            value = dot_nt(m[s, :], c[:, :wide]) + dot_nt(r[s, :], c[:, wide:])
            refs[-1][s, :] = value if before is None else value + refs[0][s, :]

    args = [stay(own), stay(other), stay(cols)] + ([] if before is None else [stay(before)])
    return call(
        kernel, "predicted", [IN_VMEM] * len(args), args, IN_VMEM, pltpu.VMEM((rows, cols.shape[0]), F32), [],
        4 * rows * cols.shape[0] * wide,
    )


def last_product(own, other, cols, before, out, part, rows):
    wide, depth = own.shape[1], cols.shape[0]
    spans = [slice(i, i + 256) for i in range(0, part.stop - part.start, 256)]
    slots = 4

    def kernel(m, r, c, *refs):
        to, held, sem = refs[-3:]
        moves = []
        for i, s in enumerate(spans):
            at = slice(part.start + s.start, part.start + s.stop)
            if i >= slots:
                moves[i - slots].wait()
            value = dot_nt(m[s, :], c[:, :wide]) + dot_nt(r[s, :], c[:, wide:])
            held[i % slots] = value if before is None else value + refs[0][at, :]
            moves.append(pltpu.make_async_copy(held.at[i % slots], to.at[at, :], sem.at[i % slots]))
            moves[i].start()
        for move in moves[-slots:]:
            move.wait()

    args = [stay(own), stay(other), stay(cols)] + ([] if before is None else [stay(before)])
    in_specs = [IN_VMEM] * len(args)
    aliases = {}
    if out is not None:
        aliases = {len(args): 0}
        args.append(leave(out))
        in_specs.append(IN_HBM)
    scratch = [pltpu.VMEM((slots, 256, depth), F32), pltpu.SemaphoreType.DMA((slots,))]
    return call(
        kernel, "predicted", in_specs, args, IN_HBM, jax.ShapeDtypeStruct((rows, depth), F32), scratch,
        4 * (part.stop - part.start) * depth * wide, aliases,
    )


def shards(nc, nt, affinity, comp_vectors, targ_vectors, comp_values, targ_values):
    cbits, tbits = nc.bit_length() - 1, nt.bit_length() - 2
    c_orders = ([1 << b for b in range(cbits)], [1 << b for b in reversed(range(cbits))])
    t_orders = ([2 << b for b in range(tbits)],) * 2
    iblock, jblock = comp_vectors.shape[1] // nc, targ_vectors.shape[1] // nt
    chunks = 2 if jblock % 256 == 0 else 1
    width = jblock // chunks

    def offset(position, order):
        return functools.reduce(lambda a, b: a ^ b, [mask for t, mask in enumerate(order) if (position >> (len(order) - 1 - t)) & 1], 0)

    def pick(orders, position, flip, core):
        return jnp.where(core == 0, offset(position, orders[flip]), offset(position, orders[1 - flip]))

    def c_blocks(p):
        return lax.axis_index("cmp") ^ pick(c_orders, p, 0, lax.axis_index("tgt") % 2)

    def keep(q):
        at = lax.axis_index("tgt")
        return at ^ pick(t_orders, q, 0, at % 2)

    def give(q):
        at = lax.axis_index("tgt")
        return at ^ 1 ^ pick(t_orders, q, 1, at % 2)

    def both(q):
        return keep(q) if q < nt // 2 else give(q - nt // 2)

    def swap_c(x, t):
        pairs = [(c * nt + i, (c ^ c_orders[i % 2][t]) * nt + i) for c in range(nc) for i in range(nt)]
        return lax.ppermute(x, ("cmp", "tgt"), pairs)

    def swap_t(x, t):
        return lax.ppermute(x, "tgt", [(i, i ^ t_orders[i % 2][t]) for i in range(nt)])

    def swap_core(x):
        return lax.ppermute(x, "tgt", [(i, i ^ 1) for i in range(nt)])

    bound = 6 * 0.0625 * 0.0546875 * affinity.shape[0] * nc * affinity.shape[1] * nt
    scale = 1.0
    while bound * scale > 65000:
        scale *= 0.5

    kinds = "c" * cbits + "t" * tbits
    steps = [(kind, kinds[:i].count(kind)) for i, kind in enumerate(kinds)]
    count = len(steps)

    def exchange(x, i):
        kind, t = steps[i]
        return swap_c(x, t) if kind == "c" else swap_t(x, t)

    def after(x, y):
        return lax.optimization_barrier((x, y))[0]

    every, upper, lower = slice(0, nt // 2), slice(nc // 2, nc), slice(0, nc // 2)
    give_cols = [(targ_vectors, give, jblock, k * width, width, every) for k in range(chunks)]
    keep_cols = [(targ_vectors, keep, jblock, k * width, width, every) for k in range(chunks)]
    vc_cols = [(comp_vectors, c_blocks, iblock, 0, iblock, part) for part in (upper, lower)]
    if chunks == 2:
        sent, y, _, given = half_product(None, None, affinity, give_cols, BF16)
        came = [swap_core(sent)]
        sent, *kept = half_product(y, given, affinity, keep_cols, BF16)
        came.append(swap_core(sent))
        mine, vc_far = half_product(y, kept[0], affinity, vc_cols[:1], F32)
    else:
        sent, y, _, *kept = half_product(None, None, affinity, give_cols + keep_cols, BF16)
        came = [swap_core(sent)]
        mine, vc_far, vc_near = half_product(y, kept[0], affinity, vc_cols, F32)
    pair_values = swap_t(targ_values, tbits - 1)
    half, far = far_product(mine, came[0], vc_far, scale)
    coming = [exchange(far.astype(F16), 0)]
    token = far
    if chunks == 2:
        mine, vc_near = half_product(after(y, far), kept[1], affinity, vc_cols[1:], F32)
        late_half, late_far = far_product(mine, came[1], vc_far, scale)
        token = late_far
    near, columns = near_product(
        after(half, token), vc_near, scale, targ_vectors, both, nt, [] if chunks == 2 else [0], jblock, width
    )
    token, nears = near, [near]
    held = list(nears)
    rows = affinity.shape[0]
    total = out = None

    def event(k, i, token):
        came = after(coming[k], token)
        if i == count - 1:
            n = came.shape[0] // 2
            came = jnp.concatenate([came[n:], came[:n]])
        if i < count:
            total = held[k] + came.astype(F32)
            if i < count - 2:
                n = total.shape[steps[i + 1][0] == "c"] // 2
                held[k], goes = (total[:, :n], total[:, n:]) if steps[i + 1][0] == "c" else (total[:n], total[n:])
            else:
                held[k] = goes = total
            if i < count - 1:
                goes = goes.astype(F16)
                coming[k] = exchange(goes, i + 1)
                return goes
            lt = jnp.concatenate([x[k * width : (k + 1) * width] for x in (targ_values, pair_values)])
            held[k] = (total * (1 / scale) / (lt[:, None] * comp_values[None, :] + 0.25)).astype(BF16)
        else:
            held[k] = jnp.concatenate([held[k], came], axis=int(steps[2 * count - 2 - i][0] == "c"))
        coming[k] = exchange(held[k], 2 * count - 3 - i)
        return held[k]

    final = 2 * count - 2
    token = event(0, 0, token)
    if chunks == 2:
        token = event(0, 1, token)
        goes = after(late_far, token).astype(F16)
        coming.append(exchange(goes, 0))
        near, columns = near_product(after(late_half, goes), vc_near, scale, targ_vectors, both, nt, [0, 1], jblock, width)
        held.append(near)
    order = [(0, i) for i in range(chunks, final + 1)]
    if chunks == 2:
        late = [(1, i) for i in range(final + 1)]
        order = ORDER if count == 4 else [x for pair in zip(order + [None], late) for x in pair if x]
    whole, parts = [slice(0, rows)], [slice(0, rows // 2), slice(rows // 2, rows)]
    for k, i in order:
        if i < final:
            token = event(k, i, token)
            if (k, i) == (chunks - 1, final - 1) and chunks > 1:
                early, _ = lax.optimization_barrier((early, token))
                total = token = middle_product(early, swap_core(early), columns[0], None)
        else:
            last = after(coming[k], token)
            mapped = [mapped_product(vc_near, vc_far, held[k], last, s) for s in (whole if k < chunks - 1 else parts)]
            early = token = mapped[0]
    for x, s in zip(mapped, parts):
        out = last_product(x, swap_core(x), columns[chunks - 1], total, out, s, rows)
    return out


def solution(mesh):
    in_specs = (P("cmp", "tgt"), P("cmp", None), P("tgt", None), P("cmp"), P("tgt"))
    out_specs = P("cmp", "tgt")
    body = functools.partial(shards, mesh.shape["cmp"], mesh.shape["tgt"])
    return jax.shard_map(body, mesh=mesh, in_specs=in_specs, out_specs=out_specs, check_vma=False)
```

```python
import functools

import jax
import jax.numpy as jnp
from jax import lax
from jax.experimental import pallas as pl
from jax.experimental.pallas import tpu as pltpu
from jax.sharding import PartitionSpec as P

F32, BF16, F16 = jnp.float32, jnp.bfloat16, jnp.float16
LIMIT = 10 * 1024 * 1024
TILE = 512
ORDER = [(0, 2), (1, 0), (0, 3), (1, 1), (0, 4), (1, 2), (0, 5), (1, 3), (1, 4), (0, 6), (1, 5), (1, 6)]
IN_VMEM = pl.BlockSpec(memory_space=pltpu.VMEM)
IN_HBM = pl.BlockSpec(memory_space=pltpu.HBM)


def stay(x):
    return pltpu.with_memory_space_constraint(x, pltpu.VMEM)


def leave(x):
    return pltpu.with_memory_space_constraint(x, pltpu.HBM)


def dot_nn(a, b):
    return jnp.dot(a, b, preferred_element_type=F32)


def dot_nt(a, b):
    return lax.dot_general(a, b, (((1,), (1,)), ((), ())), preferred_element_type=F32)


def tiles(n):
    return [slice(i, min(i + TILE, n)) for i in range(0, n, TILE)]


def call(kernel, name, in_specs, args, out_specs, out_shape, scratch, flops, aliases=None):
    return pl.pallas_call(
        kernel,
        name=name,
        in_specs=in_specs,
        out_specs=out_specs,
        out_shape=out_shape,
        scratch_shapes=scratch,
        input_output_aliases=aliases or {},
        cost_estimate=pl.CostEstimate(flops=flops // 100, bytes_accessed=0, transcendentals=0),
        compiler_params=pltpu.CompilerParams(vmem_limit_bytes=LIMIT),
    )(*args)


def column_copies(idx, source, target, block, start, width, sem):
    found = []
    for q in range(target.shape[1] // width):
        at = pl.multiple_of(idx(q) * block + start, width)
        found.append(pltpu.make_async_copy(source.at[:, pl.ds(at, width)], target.at[:, pl.ds(q * width, width)], sem.at[q]))
    return found


def half_product(y, cols, aff, fetch, dtype):
    rows, depth = aff.shape
    spans = tiles(rows)
    wide = (fetch[0][5].stop - fetch[0][5].start) * fetch[0][4] if cols is None else cols.shape[1]
    sources = []
    for f in fetch:
        if not any(f[0] is x for x in sources):
            sources.append(f[0])
    def place(x, among):
        return [i for i, z in enumerate(among) if z is x][0]

    def kernel(*refs):
        refs = list(refs)
        from_hbm = [refs.pop(0) for _ in sources]
        a = refs.pop(0)
        c = refs.pop(0) if cols is not None else None
        out = refs.pop(0)
        loads = []
        if y is None:
            source, a = a, refs.pop(0)
        got = [refs.pop(0) for _ in fetch]
        if y is None:
            y_sem = refs.pop(0)
            loads = [pltpu.make_async_copy(source.at[s, :], a.at[s, :], y_sem.at[i]) for i, s in enumerate(spans)]
        moves = []
        for f, to in zip(fetch, got):
            sem = refs.pop(0)
            group = []
            step = min(128, f[4])
            for i, q in enumerate(range(f[5].start, f[5].stop)):
                for j in range(0, f[4], step):
                    at = pl.multiple_of(f[1](q) * f[2] + f[3] + j, step)
                    part = from_hbm[place(f[0], sources)].at[:, pl.ds(at, step)]
                    here = i * f[4] + j
                    group.append(pltpu.make_async_copy(part, to.at[:, pl.ds(here, step)], sem.at[here // step]))
            moves.append(group)
        queue = [[load] for load in loads]
        if cols is None:
            queue[0] = moves[0] + queue[0]
            queue += moves[1:]
        else:
            queue += moves
        begun = 0
        for group in queue[: 2 if loads else len(queue)]:
            begun += 1
            for move in group:
                move.start()
        if cols is None:
            for move in moves[0]:
                move.wait()
            c = got[0]
        for i, s in enumerate(spans):
            if loads:
                loads[i].wait()
            if begun < len(queue):
                for move in queue[begun]:
                    move.start()
                begun += 1
            out[:, s] = dot_nn(a[s, :], c[...]).astype(dtype).T
        for group in queue[begun:]:
            for move in group:
                move.start()
        for group in moves[1:] if cols is None else moves:
            for move in group:
                move.wait()

    out_shape = [pltpu.VMEM((wide, rows), dtype)]
    args = [leave(x) for x in sources]
    in_specs = [IN_HBM] * len(sources)
    scratch = []
    if y is None:
        args.append(leave(aff))
        in_specs.append(IN_HBM)
        out_shape.append(pltpu.VMEM(aff.shape, BF16))
        scratch.append(pltpu.SemaphoreType.DMA((len(spans),)))
    else:
        args.append(stay(y))
        in_specs.append(IN_VMEM)
    if cols is not None:
        args.append(stay(cols))
        in_specs.append(IN_VMEM)
    for f in fetch:
        n = f[5].stop - f[5].start
        out_shape.append(pltpu.VMEM((f[0].shape[0], n * f[4]), BF16))
        scratch.append(pltpu.SemaphoreType.DMA((n * f[4] // min(128, f[4]),)))
    return call(
        kernel, "half", in_specs, args, [IN_VMEM] * len(out_shape), out_shape, scratch, 2 * rows * depth * wide
    )


def keep_products(y, cols, came, vc_far, vc, order, block, take, earlier, scale):
    rows, wide = y.shape[0], cols.shape[1]
    step = min(128, block)
    shapes = [(vc.shape[0], (part.stop - part.start) * block) for part in take]

    def kernel(*refs):
        refs = list(refs)
        a, c, r, v = (refs.pop(0) for _ in range(4))
        far_cols = refs.pop(0) if vc_far is not None else None
        past = refs.pop(0) if earlier is not None else None
        half, far = refs.pop(0), refs.pop(0)
        near = refs.pop(0) if earlier is not None else None
        got, sems = refs[: len(take)], refs[len(take) :]
        moves = []
        for part, to, sem in zip(take, got, sems):
            group = []
            for i, p in enumerate(range(part.start, part.stop)):
                for j in range(0, block, step):
                    here = i * block + j
                    at = pl.multiple_of(order(p) * block + j, step)
                    group.append(
                        pltpu.make_async_copy(v.at[:, pl.ds(at, step)], to.at[:, pl.ds(here, step)], sem.at[here // step])
                    )
            moves.append(group)
        for move in sum(moves, []):
            move.start()
        for s in tiles(rows):
            half[:, s] = (dot_nn(a[s, :], c[...]).T + r[:, s].astype(F32)).astype(BF16)
        if far_cols is None:
            far_cols = got[0]
            for move in moves[0]:
                move.wait()
        for t in tiles(far.shape[1]):
            far[:, t] = dot_nn(half[...], far_cols[:, t]) * scale
        for move in sum(moves[1:] if vc_far is None else moves, []):
            move.wait()
        if earlier is not None:
            for t in tiles(near.shape[1]):
                near[:, t] = dot_nn(past[...], got[-1][:, t]) * scale

    columns = vc.shape[1] // 2
    args = [stay(y), stay(cols), stay(came), leave(vc)] + [stay(x) for x in (vc_far, earlier) if x is not None]
    in_specs = [IN_VMEM] * 3 + [IN_HBM] + [IN_VMEM] * (len(args) - 4)
    out_shape = [pltpu.VMEM((wide, rows), BF16), jax.ShapeDtypeStruct((wide, columns), F32)]
    if earlier is not None:
        out_shape.append(jax.ShapeDtypeStruct((wide, columns), F32))
    out_shape += [pltpu.VMEM(shape, BF16) for shape in shapes]
    scratch = [pltpu.SemaphoreType.DMA((shape[1] // step,)) for shape in shapes]
    return call(
        kernel, "keep", in_specs, args, [IN_VMEM] * len(out_shape), out_shape, scratch, 2 * rows * wide * (y.shape[1] + columns)
    )


def near_product(half, vc, scale, vt, idx, n, wanted, block, width):
    wide, rows = half.shape
    depth = vt.shape[0]

    def kernel(h, w, v, out, *refs):
        moves = []
        for k, cols, sem in zip(wanted, refs, refs[len(wanted) :]):
            moves += column_copies(idx, v, cols, block, k * width, width, sem)
        for move in moves:
            move.start()
        for t in tiles(vc.shape[1]):
            out[:, t] = dot_nn(h[...], w[:, t]) * scale
        for move in moves:
            move.wait()

    out_shape = [jax.ShapeDtypeStruct((wide, vc.shape[1]), F32)] + [pltpu.VMEM((depth, 2 * wide), BF16)] * len(wanted)
    near, *cols = call(
        kernel, "near", [IN_VMEM] * 2 + [IN_HBM], [stay(half), stay(vc), leave(vt)],
        [IN_VMEM] * len(out_shape), out_shape, [pltpu.SemaphoreType.DMA((n,))] * len(wanted), 2 * wide * rows * vc.shape[1],
    )
    return near, cols


def mapped_product(vc_near, vc_far, near, far, part):
    rows, wide = part.stop - part.start, near.shape[0]

    def kernel(v, w, a, b, out):
        for t in tiles(rows):
            at = slice(part.start + t.start, part.start + t.stop)
            out[t, :] = (dot_nt(v[at, :], a[...]) + dot_nt(w[at, :], b[...])).astype(BF16)

    return call(
        kernel, "mapped", [IN_VMEM] * 4, [stay(vc_near), stay(vc_far), stay(near), stay(far)], IN_VMEM,
        jax.ShapeDtypeStruct((rows, wide), BF16), [], 4 * rows * vc_near.shape[1] * wide,
    )


def middle_product(own, other, cols, before):
    rows, wide = own.shape

    def kernel(m, r, c, *refs):
        for s in [slice(i, i + 256) for i in range(0, rows, 256)]:
            value = dot_nt(m[s, :], c[:, :wide]) + dot_nt(r[s, :], c[:, wide:])
            refs[-1][s, :] = value if before is None else value + refs[0][s, :]

    args = [stay(own), stay(other), stay(cols)] + ([] if before is None else [stay(before)])
    return call(
        kernel, "predicted", [IN_VMEM] * len(args), args, IN_VMEM, pltpu.VMEM((rows, cols.shape[0]), F32), [],
        4 * rows * cols.shape[0] * wide,
    )


def last_product(own, other, cols, before, out, part, rows):
    wide, depth = own.shape[1], cols.shape[0]
    spans = [slice(i, i + 256) for i in range(0, part.stop - part.start, 256)]
    slots = 4

    def kernel(m, r, c, *refs):
        to, held, sem = refs[-3:]
        moves = []
        for i, s in enumerate(spans):
            at = slice(part.start + s.start, part.start + s.stop)
            if i >= slots:
                moves[i - slots].wait()
            value = dot_nt(m[s, :], c[:, :wide]) + dot_nt(r[s, :], c[:, wide:])
            held[i % slots] = value if before is None else value + refs[0][at, :]
            moves.append(pltpu.make_async_copy(held.at[i % slots], to.at[at, :], sem.at[i % slots]))
            moves[i].start()
        for move in moves[-slots:]:
            move.wait()

    args = [stay(own), stay(other), stay(cols)] + ([] if before is None else [stay(before)])
    in_specs = [IN_VMEM] * len(args)
    aliases = {}
    if out is not None:
        aliases = {len(args): 0}
        args.append(leave(out))
        in_specs.append(IN_HBM)
    scratch = [pltpu.VMEM((slots, 256, depth), F32), pltpu.SemaphoreType.DMA((slots,))]
    return call(
        kernel, "predicted", in_specs, args, IN_HBM, jax.ShapeDtypeStruct((rows, depth), F32), scratch,
        4 * (part.stop - part.start) * depth * wide, aliases,
    )


def shards(nc, nt, affinity, comp_vectors, targ_vectors, comp_values, targ_values):
    cbits, tbits = nc.bit_length() - 1, nt.bit_length() - 2
    c_orders = ([1 << b for b in range(cbits)], [1 << b for b in reversed(range(cbits))])
    t_orders = ([2 << b for b in range(tbits)],) * 2
    iblock, jblock = comp_vectors.shape[1] // nc, targ_vectors.shape[1] // nt
    chunks = 2 if jblock % 256 == 0 else 1
    width = jblock // chunks

    def offset(position, order):
        return functools.reduce(lambda a, b: a ^ b, [mask for t, mask in enumerate(order) if (position >> (len(order) - 1 - t)) & 1], 0)

    def pick(orders, position, flip, core):
        return jnp.where(core == 0, offset(position, orders[flip]), offset(position, orders[1 - flip]))

    def c_blocks(p):
        return lax.axis_index("cmp") ^ pick(c_orders, p, 0, lax.axis_index("tgt") % 2)

    def keep(q):
        at = lax.axis_index("tgt")
        return at ^ pick(t_orders, q, 0, at % 2)

    def give(q):
        at = lax.axis_index("tgt")
        return at ^ 1 ^ pick(t_orders, q, 1, at % 2)

    def both(q):
        return keep(q) if q < nt // 2 else give(q - nt // 2)

    def swap_c(x, t):
        pairs = [(c * nt + i, (c ^ c_orders[i % 2][t]) * nt + i) for c in range(nc) for i in range(nt)]
        return lax.ppermute(x, ("cmp", "tgt"), pairs)

    def swap_t(x, t):
        return lax.ppermute(x, "tgt", [(i, i ^ t_orders[i % 2][t]) for i in range(nt)])

    def swap_core(x):
        return lax.ppermute(x, "tgt", [(i, i ^ 1) for i in range(nt)])

    bound = 6 * 0.0625 * 0.0546875 * affinity.shape[0] * nc * affinity.shape[1] * nt
    scale = 1.0
    while bound * scale > 65000:
        scale *= 0.5

    kinds = "c" * cbits + "t" * tbits
    steps = [(kind, kinds[:i].count(kind)) for i, kind in enumerate(kinds)]
    count = len(steps)

    def exchange(x, i):
        kind, t = steps[i]
        return swap_c(x, t) if kind == "c" else swap_t(x, t)

    def after(x, y):
        return lax.optimization_barrier((x, y))[0]

    every, upper, lower = slice(0, nt // 2), slice(nc // 2, nc), slice(0, nc // 2)
    give_cols = [(targ_vectors, give, jblock, k * width, width, every) for k in range(chunks)]
    keep_cols = [(targ_vectors, keep, jblock, k * width, width, every) for k in range(chunks)]
    if chunks == 2:
        sent, y, _, given = half_product(None, None, affinity, give_cols, BF16)
        came = [swap_core(sent)]
        sent, *kept = half_product(y, given, affinity, keep_cols, BF16)
        came.append(swap_core(sent))
        half, far, vc_far = keep_products(y, kept[0], came[0], None, comp_vectors, c_blocks, iblock, [upper], None, scale)
    else:
        sent, y, _, *kept = half_product(None, None, affinity, give_cols + keep_cols, BF16)
        came = [swap_core(sent)]
        half, far, vc_far, vc_near = keep_products(
            y, kept[0], came[0], None, comp_vectors, c_blocks, iblock, [upper, lower], None, scale
        )
    coming = [exchange(far.astype(F16), 0)]
    if chunks == 2:
        late_half, late_far, near, vc_near = keep_products(
            after(y, far), kept[1], came[1], vc_far, comp_vectors, c_blocks, iblock, [lower], half, scale
        )
    else:
        near, columns = near_product(half, vc_near, scale, targ_vectors, both, nt, [0], jblock, width)
    token, nears = near, [near]
    held = list(nears)
    rows = affinity.shape[0]
    total = out = None

    def event(k, i, token):
        came = after(coming[k], token)
        if i == count - 1:
            n = came.shape[0] // 2
            came = jnp.concatenate([came[n:], came[:n]])
        if i < count:
            total = held[k] + came.astype(F32)
            if i < count - 2:
                n = total.shape[steps[i + 1][0] == "c"] // 2
                held[k], goes = (total[:, :n], total[:, n:]) if steps[i + 1][0] == "c" else (total[:n], total[n:])
            else:
                held[k] = goes = total
            if i < count - 1:
                goes = goes.astype(F16)
                coming[k] = exchange(goes, i + 1)
                return goes
            lt = lts[:, k * width : (k + 1) * width, None]
            total = total.reshape(2, width, -1) * (1 / scale) / (lt * comp_values[None, None, :] + 0.25)
            held[k] = total.astype(BF16).reshape(2 * width, -1)
        else:
            held[k] = jnp.concatenate([held[k], came], axis=int(steps[2 * count - 2 - i][0] == "c"))
        coming[k] = exchange(held[k], 2 * count - 3 - i)
        return held[k]

    final = 2 * count - 2
    token = event(0, 0, token)
    pair_values = swap_t(after(targ_values, token), tbits - 1)
    lts = jnp.stack([targ_values, pair_values])
    if chunks == 2:
        coming[0], lts = lax.optimization_barrier((coming[0], lts))
        token = event(0, 1, token)
        goes = after(late_far, token).astype(F16)
        coming.append(exchange(goes, 0))
        near, columns = near_product(after(late_half, goes), vc_near, scale, targ_vectors, both, nt, [0, 1], jblock, width)
        held.append(near)
    order = [(0, i) for i in range(chunks, final + 1)]
    if chunks == 2:
        late = [(1, i) for i in range(final + 1)]
        order = ORDER if count == 4 else [x for pair in zip(order + [None], late) for x in pair if x]
    whole, parts = [slice(0, rows)], [slice(0, rows // 2), slice(rows // 2, rows)]
    for k, i in order:
        if i < final:
            token = event(k, i, token)
            if (k, i) == (chunks - 1, final - 1) and chunks > 1:
                early, _ = lax.optimization_barrier((early, token))
                total = token = middle_product(early, swap_core(early), columns[0], None)
        else:
            last = after(coming[k], token)
            mapped = [mapped_product(vc_near, vc_far, held[k], last, s) for s in (whole if k < chunks - 1 else parts)]
            early = token = mapped[0]
    for x, s in zip(mapped, parts):
        out = last_product(x, swap_core(x), columns[chunks - 1], total, out, s, rows)
    return out


def solution(mesh):
    in_specs = (P("cmp", "tgt"), P("cmp", None), P("tgt", None), P("cmp"), P("tgt"))
    out_specs = P("cmp", "tgt")
    body = functools.partial(shards, mesh.shape["cmp"], mesh.shape["tgt"])
    return jax.shard_map(body, mesh=mesh, in_specs=in_specs, out_specs=out_specs, check_vma=False)
```

```python
import functools

import jax
import jax.numpy as jnp
from jax import lax
from jax.experimental import pallas as pl
from jax.experimental.pallas import tpu as pltpu
from jax.sharding import PartitionSpec as P

F32, BF16, F16 = jnp.float32, jnp.bfloat16, jnp.float16
LIMIT = 10 * 1024 * 1024
TILE = 512
ORDER = [(0, 2), (1, 0), (0, 3), (1, 1), (0, 4), (1, 2), (0, 5), (1, 3), (1, 4), (0, 6), (1, 5), (1, 6)]
IN_VMEM = pl.BlockSpec(memory_space=pltpu.VMEM)
IN_HBM = pl.BlockSpec(memory_space=pltpu.HBM)


def stay(x):
    return pltpu.with_memory_space_constraint(x, pltpu.VMEM)


def leave(x):
    return pltpu.with_memory_space_constraint(x, pltpu.HBM)


def dot_nn(a, b):
    return jnp.dot(a, b, preferred_element_type=F32)


def dot_nt(a, b):
    return lax.dot_general(a, b, (((1,), (1,)), ((), ())), preferred_element_type=F32)


def tiles(n):
    return [slice(i, min(i + TILE, n)) for i in range(0, n, TILE)]


def call(kernel, name, in_specs, args, out_specs, out_shape, scratch, flops, aliases=None):
    return pl.pallas_call(
        kernel,
        name=name,
        in_specs=in_specs,
        out_specs=out_specs,
        out_shape=out_shape,
        scratch_shapes=scratch,
        input_output_aliases=aliases or {},
        cost_estimate=pl.CostEstimate(flops=flops // 100, bytes_accessed=0, transcendentals=0),
        compiler_params=pltpu.CompilerParams(vmem_limit_bytes=LIMIT),
    )(*args)


def column_copies(idx, source, target, block, start, width, sem):
    found = []
    for q in range(target.shape[1] // width):
        at = pl.multiple_of(idx(q) * block + start, width)
        found.append(pltpu.make_async_copy(source.at[:, pl.ds(at, width)], target.at[:, pl.ds(q * width, width)], sem.at[q]))
    return found


def half_product(y, cols, aff, fetch, dtype):
    rows, depth = aff.shape
    spans = tiles(rows)
    wide = (fetch[0][5].stop - fetch[0][5].start) * fetch[0][4] if cols is None else cols.shape[1]
    sources = []
    for f in fetch:
        if not any(f[0] is x for x in sources):
            sources.append(f[0])
    def place(x, among):
        return [i for i, z in enumerate(among) if z is x][0]

    def kernel(*refs):
        refs = list(refs)
        from_hbm = [refs.pop(0) for _ in sources]
        a = refs.pop(0)
        c = refs.pop(0) if cols is not None else None
        out = refs.pop(0)
        loads = []
        if y is None:
            source, a = a, refs.pop(0)
        got = [refs.pop(0) for _ in fetch]
        if y is None:
            y_sem = refs.pop(0)
            loads = [pltpu.make_async_copy(source.at[s, :], a.at[s, :], y_sem.at[i]) for i, s in enumerate(spans)]
        moves = []
        for f, to in zip(fetch, got):
            sem = refs.pop(0)
            group = []
            step = min(128, f[4])
            for i, q in enumerate(range(f[5].start, f[5].stop)):
                for j in range(0, f[4], step):
                    at = pl.multiple_of(f[1](q) * f[2] + f[3] + j, step)
                    part = from_hbm[place(f[0], sources)].at[:, pl.ds(at, step)]
                    here = i * f[4] + j
                    group.append(pltpu.make_async_copy(part, to.at[:, pl.ds(here, step)], sem.at[here // step]))
            moves.append(group)
        queue = [[load] for load in loads]
        if cols is None:
            queue[0] = moves[0] + queue[0]
            queue += moves[1:]
        else:
            queue += moves
        begun = 0
        for group in queue[: 2 if loads else len(queue)]:
            begun += 1
            for move in group:
                move.start()
        if cols is None:
            for move in moves[0]:
                move.wait()
            c = got[0]
        for i, s in enumerate(spans):
            if loads:
                loads[i].wait()
            if begun < len(queue):
                for move in queue[begun]:
                    move.start()
                begun += 1
            out[:, s] = dot_nn(a[s, :], c[...]).astype(dtype).T
        for group in queue[begun:]:
            for move in group:
                move.start()
        for group in moves[1:] if cols is None else moves:
            for move in group:
                move.wait()

    out_shape = [pltpu.VMEM((wide, rows), dtype)]
    args = [leave(x) for x in sources]
    in_specs = [IN_HBM] * len(sources)
    scratch = []
    if y is None:
        args.append(leave(aff))
        in_specs.append(IN_HBM)
        out_shape.append(pltpu.VMEM(aff.shape, BF16))
        scratch.append(pltpu.SemaphoreType.DMA((len(spans),)))
    else:
        args.append(stay(y))
        in_specs.append(IN_VMEM)
    if cols is not None:
        args.append(stay(cols))
        in_specs.append(IN_VMEM)
    for f in fetch:
        n = f[5].stop - f[5].start
        out_shape.append(pltpu.VMEM((f[0].shape[0], n * f[4]), BF16))
        scratch.append(pltpu.SemaphoreType.DMA((n * f[4] // min(128, f[4]),)))
    return call(
        kernel, "half", in_specs, args, [IN_VMEM] * len(out_shape), out_shape, scratch, 2 * rows * depth * wide
    )


def keep_products(y, cols, came, vc_far, vc, order, block, take, earlier, scale):
    rows, wide = y.shape[0], cols.shape[1]
    step = min(128, block)
    shapes = [(vc.shape[0], (part.stop - part.start) * block) for part in take]

    def kernel(*refs):
        refs = list(refs)
        a, c, r, v = (refs.pop(0) for _ in range(4))
        far_cols = refs.pop(0) if vc_far is not None else None
        past = refs.pop(0) if earlier is not None else None
        half, far = refs.pop(0), refs.pop(0)
        near = refs.pop(0) if earlier is not None else None
        got, sems = refs[: len(take)], refs[len(take) :]
        moves = []
        for part, to, sem in zip(take, got, sems):
            group = []
            for i, p in enumerate(range(part.start, part.stop)):
                for j in range(0, block, step):
                    here = i * block + j
                    at = pl.multiple_of(order(p) * block + j, step)
                    group.append(
                        pltpu.make_async_copy(v.at[:, pl.ds(at, step)], to.at[:, pl.ds(here, step)], sem.at[here // step])
                    )
            moves.append(group)
        for move in sum(moves, []):
            move.start()
        for s in tiles(rows):
            half[:, s] = (dot_nn(a[s, :], c[...]).T + r[:, s].astype(F32)).astype(BF16)
        if far_cols is None:
            far_cols = got[0]
            for move in moves[0]:
                move.wait()
        for t in tiles(far.shape[1]):
            far[:, t] = dot_nn(half[...], far_cols[:, t]) * scale
        for move in sum(moves[1:] if vc_far is None else moves, []):
            move.wait()
        if earlier is not None:
            for t in tiles(near.shape[1]):
                near[:, t] = dot_nn(past[...], got[-1][:, t]) * scale

    columns = vc.shape[1] // 2
    args = [stay(y), stay(cols), stay(came), leave(vc)] + [stay(x) for x in (vc_far, earlier) if x is not None]
    in_specs = [IN_VMEM] * 3 + [IN_HBM] + [IN_VMEM] * (len(args) - 4)
    out_shape = [pltpu.VMEM((wide, rows), BF16), jax.ShapeDtypeStruct((wide, columns), F32)]
    if earlier is not None:
        out_shape.append(jax.ShapeDtypeStruct((wide, columns), F32))
    out_shape += [pltpu.VMEM(shape, BF16) for shape in shapes]
    scratch = [pltpu.SemaphoreType.DMA((shape[1] // step,)) for shape in shapes]
    return call(
        kernel, "keep", in_specs, args, [IN_VMEM] * len(out_shape), out_shape, scratch, 2 * rows * wide * (y.shape[1] + columns)
    )


def near_product(half, vc, scale, vt, idx, n, wanted, block, width):
    wide, rows = half.shape
    depth = vt.shape[0]

    def kernel(h, w, v, out, *refs):
        moves = []
        for k, cols, sem in zip(wanted, refs, refs[len(wanted) :]):
            moves += column_copies(idx, v, cols, block, k * width, width, sem)
        for move in moves:
            move.start()
        for t in tiles(vc.shape[1]):
            out[:, t] = dot_nn(h[...], w[:, t]) * scale
        for move in moves:
            move.wait()

    out_shape = [jax.ShapeDtypeStruct((wide, vc.shape[1]), F32)] + [pltpu.VMEM((depth, 2 * wide), BF16)] * len(wanted)
    near, *cols = call(
        kernel, "near", [IN_VMEM] * 2 + [IN_HBM], [stay(half), stay(vc), leave(vt)],
        [IN_VMEM] * len(out_shape), out_shape, [pltpu.SemaphoreType.DMA((n,))] * len(wanted), 2 * wide * rows * vc.shape[1],
    )
    return near, cols


def mapped_product(vc_near, vc_far, near, far, part):
    rows, wide = part.stop - part.start, near.shape[0]

    def kernel(v, w, a, b, out):
        for t in tiles(rows):
            at = slice(part.start + t.start, part.start + t.stop)
            out[t, :] = (dot_nt(v[at, :], a[...]) + dot_nt(w[at, :], b[...])).astype(BF16)

    return call(
        kernel, "mapped", [IN_VMEM] * 4, [stay(vc_near), stay(vc_far), stay(near), stay(far)], IN_VMEM,
        jax.ShapeDtypeStruct((rows, wide), BF16), [], 4 * rows * vc_near.shape[1] * wide,
    )


def part_product(vc, near):
    rows, wide = vc.shape[0], near.shape[0]

    def kernel(v, a, out):
        for t in tiles(rows):
            out[t, :] = dot_nt(v[t, :], a[...])

    return call(
        kernel, "part", [IN_VMEM] * 2, [stay(vc), stay(near)], IN_VMEM, pltpu.VMEM((rows, wide), F32), [],
        2 * rows * vc.shape[1] * wide,
    )


def rest_product(before, vc, far, part):
    rows, wide = part.stop - part.start, far.shape[0]

    def kernel(b, w, a, out):
        for t in tiles(rows):
            at = slice(part.start + t.start, part.start + t.stop)
            out[t, :] = (b[at, :] + dot_nt(w[at, :], a[...])).astype(BF16)

    return call(
        kernel, "rest", [IN_VMEM] * 3, [stay(before), stay(vc), stay(far)], IN_VMEM, jax.ShapeDtypeStruct((rows, wide), BF16), [],
        2 * rows * vc.shape[1] * wide,
    )


def middle_product(own, other, cols, before):
    rows, wide = own.shape

    def kernel(m, r, c, *refs):
        for s in [slice(i, i + 256) for i in range(0, rows, 256)]:
            value = dot_nt(m[s, :], c[:, :wide]) + dot_nt(r[s, :], c[:, wide:])
            refs[-1][s, :] = value if before is None else value + refs[0][s, :]

    args = [stay(own), stay(other), stay(cols)] + ([] if before is None else [stay(before)])
    return call(
        kernel, "predicted", [IN_VMEM] * len(args), args, IN_VMEM, pltpu.VMEM((rows, cols.shape[0]), F32), [],
        4 * rows * cols.shape[0] * wide,
    )


def last_product(own, other, cols, before, out, part, rows):
    wide, depth = own.shape[1], cols.shape[0]
    spans = [slice(i, i + 256) for i in range(0, part.stop - part.start, 256)]
    slots = 4

    def kernel(m, r, c, *refs):
        to, held, sem = refs[-3:]
        moves = []
        for i, s in enumerate(spans):
            at = slice(part.start + s.start, part.start + s.stop)
            if i >= slots:
                moves[i - slots].wait()
            value = dot_nt(m[s, :], c[:, :wide]) + dot_nt(r[s, :], c[:, wide:])
            held[i % slots] = value if before is None else value + refs[0][at, :]
            moves.append(pltpu.make_async_copy(held.at[i % slots], to.at[at, :], sem.at[i % slots]))
            moves[i].start()
        for move in moves[-slots:]:
            move.wait()

    args = [stay(own), stay(other), stay(cols)] + ([] if before is None else [stay(before)])
    in_specs = [IN_VMEM] * len(args)
    aliases = {}
    if out is not None:
        aliases = {len(args): 0}
        args.append(leave(out))
        in_specs.append(IN_HBM)
    scratch = [pltpu.VMEM((slots, 256, depth), F32), pltpu.SemaphoreType.DMA((slots,))]
    return call(
        kernel, "predicted", in_specs, args, IN_HBM, jax.ShapeDtypeStruct((rows, depth), F32), scratch,
        4 * (part.stop - part.start) * depth * wide, aliases,
    )


def shards(nc, nt, affinity, comp_vectors, targ_vectors, comp_values, targ_values):
    cbits, tbits = nc.bit_length() - 1, nt.bit_length() - 2
    c_orders = ([1 << b for b in range(cbits)], [1 << b for b in reversed(range(cbits))])
    t_orders = ([2 << b for b in range(tbits)],) * 2
    iblock, jblock = comp_vectors.shape[1] // nc, targ_vectors.shape[1] // nt
    chunks = 2 if jblock % 256 == 0 else 1
    width = jblock // chunks

    def offset(position, order):
        return functools.reduce(lambda a, b: a ^ b, [mask for t, mask in enumerate(order) if (position >> (len(order) - 1 - t)) & 1], 0)

    def pick(orders, position, flip, core):
        return jnp.where(core == 0, offset(position, orders[flip]), offset(position, orders[1 - flip]))

    def c_blocks(p):
        return lax.axis_index("cmp") ^ pick(c_orders, p, 0, lax.axis_index("tgt") % 2)

    def keep(q):
        at = lax.axis_index("tgt")
        return at ^ pick(t_orders, q, 0, at % 2)

    def give(q):
        at = lax.axis_index("tgt")
        return at ^ 1 ^ pick(t_orders, q, 1, at % 2)

    def both(q):
        return keep(q) if q < nt // 2 else give(q - nt // 2)

    def swap_c(x, t):
        pairs = [(c * nt + i, (c ^ c_orders[i % 2][t]) * nt + i) for c in range(nc) for i in range(nt)]
        return lax.ppermute(x, ("cmp", "tgt"), pairs)

    def swap_t(x, t):
        return lax.ppermute(x, "tgt", [(i, i ^ t_orders[i % 2][t]) for i in range(nt)])

    def swap_core(x):
        return lax.ppermute(x, "tgt", [(i, i ^ 1) for i in range(nt)])

    bound = 6 * 0.0625 * 0.0546875 * affinity.shape[0] * nc * affinity.shape[1] * nt
    scale = 1.0
    while bound * scale > 65000:
        scale *= 0.5

    kinds = "c" * cbits + "t" * tbits
    steps = [(kind, kinds[:i].count(kind)) for i, kind in enumerate(kinds)]
    count = len(steps)

    def exchange(x, i):
        kind, t = steps[i]
        return swap_c(x, t) if kind == "c" else swap_t(x, t)

    def after(x, y):
        return lax.optimization_barrier((x, y))[0]

    every, upper, lower = slice(0, nt // 2), slice(nc // 2, nc), slice(0, nc // 2)
    give_cols = [(targ_vectors, give, jblock, k * width, width, every) for k in range(chunks)]
    keep_cols = [(targ_vectors, keep, jblock, k * width, width, every) for k in range(chunks)]
    if chunks == 2:
        sent, y, _, given = half_product(None, None, affinity, give_cols, BF16)
        came = [swap_core(sent)]
        sent, *kept = half_product(y, given, affinity, keep_cols, BF16)
        came.append(swap_core(sent))
        half, far, vc_far = keep_products(y, kept[0], came[0], None, comp_vectors, c_blocks, iblock, [upper], None, scale)
    else:
        sent, y, _, *kept = half_product(None, None, affinity, give_cols + keep_cols, BF16)
        came = [swap_core(sent)]
        half, far, vc_far, vc_near = keep_products(
            y, kept[0], came[0], None, comp_vectors, c_blocks, iblock, [upper, lower], None, scale
        )
    coming = [exchange(far.astype(F16), 0)]
    if chunks == 2:
        late_half, late_far, near, vc_near = keep_products(
            after(y, far), kept[1], came[1], vc_far, comp_vectors, c_blocks, iblock, [lower], half, scale
        )
    else:
        near, columns = near_product(half, vc_near, scale, targ_vectors, both, nt, [0], jblock, width)
    token, nears = near, [near]
    held = list(nears)
    rows = affinity.shape[0]
    total = out = begun = None

    def event(k, i, token):
        came = after(coming[k], token)
        if i == count - 1:
            n = came.shape[0] // 2
            came = jnp.concatenate([came[n:], came[:n]])
        if i < count:
            total = held[k] + came.astype(F32)
            if i < count - 2:
                n = total.shape[steps[i + 1][0] == "c"] // 2
                held[k], goes = (total[:, :n], total[:, n:]) if steps[i + 1][0] == "c" else (total[:n], total[n:])
            else:
                held[k] = goes = total
            if i < count - 1:
                goes = goes.astype(F16)
                coming[k] = exchange(goes, i + 1)
                return goes
            lt = lts[:, k * width : (k + 1) * width, None]
            total = total.reshape(2, width, -1) * (1 / scale) / (lt * comp_values[None, None, :] + 0.25)
            held[k] = total.astype(BF16).reshape(2 * width, -1)
        else:
            held[k] = jnp.concatenate([held[k], came], axis=int(steps[2 * count - 2 - i][0] == "c"))
        coming[k] = exchange(held[k], 2 * count - 3 - i)
        return held[k]

    final = 2 * count - 2
    token = event(0, 0, token)
    pair_values = swap_t(after(targ_values, token), tbits - 1)
    lts = jnp.stack([targ_values, pair_values])
    if chunks == 2:
        coming[0], lts = lax.optimization_barrier((coming[0], lts))
        token = event(0, 1, token)
        goes = after(late_far, token).astype(F16)
        coming.append(exchange(goes, 0))
        near, columns = near_product(after(late_half, goes), vc_near, scale, targ_vectors, both, nt, [0, 1], jblock, width)
        held.append(near)
    order = [(0, i) for i in range(chunks, final + 1)]
    if chunks == 2:
        late = [(1, i) for i in range(final + 1)]
        order = ORDER if count == 4 else [x for pair in zip(order + [None], late) for x in pair if x]
    whole, parts = [slice(0, rows)], [slice(0, rows // 2), slice(rows // 2, rows)]
    for k, i in order:
        if i < final:
            token = event(k, i, token)
            if (k, i) == (chunks - 1, final - 1) and chunks > 1:
                early, _ = lax.optimization_barrier((early, token))
                other = swap_core(early)
                other, begun = lax.optimization_barrier((other, part_product(vc_near, held[k])))
                total = token = middle_product(early, other, columns[0], None)
        else:
            last = after(coming[k], token)
            if k < chunks - 1:
                mapped = [mapped_product(vc_near, vc_far, held[k], last, s) for s in whole]
            else:
                begun = part_product(vc_near, held[k]) if begun is None else begun
                mapped = [rest_product(begun, vc_far, last, s) for s in parts]
            early = token = mapped[0]
    for x, s in zip(mapped, parts):
        out = last_product(x, swap_core(x), columns[chunks - 1], total, out, s, rows)
    return out


def solution(mesh):
    in_specs = (P("cmp", "tgt"), P("cmp", None), P("tgt", None), P("cmp"), P("tgt"))
    out_specs = P("cmp", "tgt")
    body = functools.partial(shards, mesh.shape["cmp"], mesh.shape["tgt"])
    return jax.shard_map(body, mesh=mesh, in_specs=in_specs, out_specs=out_specs, check_vma=False)
```

```python
import functools

import jax
import jax.numpy as jnp
from jax import lax
from jax.experimental import pallas as pl
from jax.experimental.pallas import tpu as pltpu
from jax.sharding import PartitionSpec as P

F32, BF16, F16 = jnp.float32, jnp.bfloat16, jnp.float16
LIMIT = 10 * 1024 * 1024
TILE = 512
ORDER = [(0, 2), (1, 0), (0, 3), (1, 1), (0, 4), (1, 2), (0, 5), (1, 3), (1, 4), (0, 6), (1, 5), (1, 6)]
IN_VMEM = pl.BlockSpec(memory_space=pltpu.VMEM)
IN_HBM = pl.BlockSpec(memory_space=pltpu.HBM)


def stay(x):
    return pltpu.with_memory_space_constraint(x, pltpu.VMEM)


def leave(x):
    return pltpu.with_memory_space_constraint(x, pltpu.HBM)


def dot_nn(a, b):
    return jnp.dot(a, b, preferred_element_type=F32)


def dot_nt(a, b):
    return lax.dot_general(a, b, (((1,), (1,)), ((), ())), preferred_element_type=F32)


def tiles(n):
    return [slice(i, min(i + TILE, n)) for i in range(0, n, TILE)]


def call(kernel, name, in_specs, args, out_specs, out_shape, scratch, flops, aliases=None):
    return pl.pallas_call(
        kernel,
        name=name,
        in_specs=in_specs,
        out_specs=out_specs,
        out_shape=out_shape,
        scratch_shapes=scratch,
        input_output_aliases=aliases or {},
        cost_estimate=pl.CostEstimate(flops=flops // 100, bytes_accessed=0, transcendentals=0),
        compiler_params=pltpu.CompilerParams(vmem_limit_bytes=LIMIT),
    )(*args)


def column_copies(idx, source, target, block, start, width, sem):
    found = []
    for q in range(target.shape[1] // width):
        at = pl.multiple_of(idx(q) * block + start, width)
        found.append(pltpu.make_async_copy(source.at[:, pl.ds(at, width)], target.at[:, pl.ds(q * width, width)], sem.at[q]))
    return found


def half_product(y, cols, aff, fetch, dtype):
    rows, depth = aff.shape
    spans = tiles(rows)
    wide = (fetch[0][5].stop - fetch[0][5].start) * fetch[0][4] if cols is None else cols.shape[1]
    sources = []
    for f in fetch:
        if not any(f[0] is x for x in sources):
            sources.append(f[0])
    def place(x, among):
        return [i for i, z in enumerate(among) if z is x][0]

    def kernel(*refs):
        refs = list(refs)
        from_hbm = [refs.pop(0) for _ in sources]
        a = refs.pop(0)
        c = refs.pop(0) if cols is not None else None
        out = refs.pop(0)
        loads = []
        if y is None:
            source, a = a, refs.pop(0)
        got = [refs.pop(0) for _ in fetch]
        if y is None:
            y_sem = refs.pop(0)
            loads = [pltpu.make_async_copy(source.at[s, :], a.at[s, :], y_sem.at[i]) for i, s in enumerate(spans)]
        moves = []
        for f, to in zip(fetch, got):
            sem = refs.pop(0)
            group = []
            step = min(128, f[4])
            for i, q in enumerate(range(f[5].start, f[5].stop)):
                for j in range(0, f[4], step):
                    at = pl.multiple_of(f[1](q) * f[2] + f[3] + j, step)
                    part = from_hbm[place(f[0], sources)].at[:, pl.ds(at, step)]
                    here = i * f[4] + j
                    group.append(pltpu.make_async_copy(part, to.at[:, pl.ds(here, step)], sem.at[here // step]))
            moves.append(group)
        queue = [[load] for load in loads]
        if cols is None:
            queue[0] = moves[0] + queue[0]
            queue += moves[1:]
        else:
            queue += moves
        begun = 0
        for group in queue[: 2 if loads else len(queue)]:
            begun += 1
            for move in group:
                move.start()
        if cols is None:
            for move in moves[0]:
                move.wait()
            c = got[0]
        for i, s in enumerate(spans):
            if loads:
                loads[i].wait()
            if begun < len(queue):
                for move in queue[begun]:
                    move.start()
                begun += 1
            out[:, s] = dot_nn(a[s, :], c[...]).astype(dtype).T
        for group in queue[begun:]:
            for move in group:
                move.start()
        for group in moves[1:] if cols is None else moves:
            for move in group:
                move.wait()

    out_shape = [pltpu.VMEM((wide, rows), dtype)]
    args = [leave(x) for x in sources]
    in_specs = [IN_HBM] * len(sources)
    scratch = []
    if y is None:
        args.append(leave(aff))
        in_specs.append(IN_HBM)
        out_shape.append(pltpu.VMEM(aff.shape, BF16))
        scratch.append(pltpu.SemaphoreType.DMA((len(spans),)))
    else:
        args.append(stay(y))
        in_specs.append(IN_VMEM)
    if cols is not None:
        args.append(stay(cols))
        in_specs.append(IN_VMEM)
    for f in fetch:
        n = f[5].stop - f[5].start
        out_shape.append(pltpu.VMEM((f[0].shape[0], n * f[4]), BF16))
        scratch.append(pltpu.SemaphoreType.DMA((n * f[4] // min(128, f[4]),)))
    return call(
        kernel, "half", in_specs, args, [IN_VMEM] * len(out_shape), out_shape, scratch, 2 * rows * depth * wide
    )


def keep_products(y, cols, came, vc_far, vc, order, block, take, earlier, scale):
    rows, wide = y.shape[0], cols.shape[1]
    step = min(128, block)
    shapes = [(vc.shape[0], (part.stop - part.start) * block) for part in take]

    def kernel(*refs):
        refs = list(refs)
        a, c, r, v = (refs.pop(0) for _ in range(4))
        far_cols = refs.pop(0) if vc_far is not None else None
        past = refs.pop(0) if earlier is not None else None
        half, far = refs.pop(0), refs.pop(0)
        near = refs.pop(0) if earlier is not None else None
        got, sems = refs[: len(take)], refs[len(take) :]
        moves = []
        for part, to, sem in zip(take, got, sems):
            group = []
            for i, p in enumerate(range(part.start, part.stop)):
                for j in range(0, block, step):
                    here = i * block + j
                    at = pl.multiple_of(order(p) * block + j, step)
                    group.append(
                        pltpu.make_async_copy(v.at[:, pl.ds(at, step)], to.at[:, pl.ds(here, step)], sem.at[here // step])
                    )
            moves.append(group)
        for move in sum(moves, []):
            move.start()
        for s in tiles(rows):
            half[:, s] = (dot_nn(a[s, :], c[...]).T + r[:, s].astype(F32)).astype(BF16)
        if far_cols is None:
            far_cols = got[0]
        for t in tiles(far.shape[1]):
            if vc_far is None:
                for move in moves[0][t.start // step : t.stop // step]:
                    move.wait()
            far[:, t] = dot_nn(half[...], far_cols[:, t]) * scale
        for move in sum(moves[1:] if vc_far is None else moves, []):
            move.wait()
        if earlier is not None:
            for t in tiles(near.shape[1]):
                near[:, t] = dot_nn(past[...], got[-1][:, t]) * scale

    columns = vc.shape[1] // 2
    args = [stay(y), stay(cols), stay(came), leave(vc)] + [stay(x) for x in (vc_far, earlier) if x is not None]
    in_specs = [IN_VMEM] * 3 + [IN_HBM] + [IN_VMEM] * (len(args) - 4)
    out_shape = [pltpu.VMEM((wide, rows), BF16), jax.ShapeDtypeStruct((wide, columns), F32)]
    if earlier is not None:
        out_shape.append(jax.ShapeDtypeStruct((wide, columns), F32))
    out_shape += [pltpu.VMEM(shape, BF16) for shape in shapes]
    scratch = [pltpu.SemaphoreType.DMA((shape[1] // step,)) for shape in shapes]
    return call(
        kernel, "keep", in_specs, args, [IN_VMEM] * len(out_shape), out_shape, scratch, 2 * rows * wide * (y.shape[1] + columns)
    )


def near_product(half, vc, scale, vt, idx, n, wanted, block, width):
    wide, rows = half.shape
    depth = vt.shape[0]

    def kernel(h, w, v, out, *refs):
        moves = []
        for k, cols, sem in zip(wanted, refs, refs[len(wanted) :]):
            moves += column_copies(idx, v, cols, block, k * width, width, sem)
        for move in moves:
            move.start()
        for t in tiles(vc.shape[1]):
            out[:, t] = dot_nn(h[...], w[:, t]) * scale
        for move in moves:
            move.wait()

    out_shape = [jax.ShapeDtypeStruct((wide, vc.shape[1]), F32)] + [pltpu.VMEM((depth, 2 * wide), BF16)] * len(wanted)
    near, *cols = call(
        kernel, "near", [IN_VMEM] * 2 + [IN_HBM], [stay(half), stay(vc), leave(vt)],
        [IN_VMEM] * len(out_shape), out_shape, [pltpu.SemaphoreType.DMA((n,))] * len(wanted), 2 * wide * rows * vc.shape[1],
    )
    return near, cols


def mapped_product(vc_near, vc_far, near, far, part):
    rows, wide = part.stop - part.start, near.shape[0]

    def kernel(v, w, a, b, out):
        for t in tiles(rows):
            at = slice(part.start + t.start, part.start + t.stop)
            out[t, :] = (dot_nt(v[at, :], a[...]) + dot_nt(w[at, :], b[...])).astype(BF16)

    return call(
        kernel, "mapped", [IN_VMEM] * 4, [stay(vc_near), stay(vc_far), stay(near), stay(far)], IN_VMEM,
        jax.ShapeDtypeStruct((rows, wide), BF16), [], 4 * rows * vc_near.shape[1] * wide,
    )


def part_product(vc, near):
    rows, wide = vc.shape[0], near.shape[0]

    def kernel(v, a, out):
        for t in tiles(rows):
            out[t, :] = dot_nt(v[t, :], a[...])

    return call(
        kernel, "part", [IN_VMEM] * 2, [stay(vc), stay(near)], IN_VMEM, pltpu.VMEM((rows, wide), F32), [],
        2 * rows * vc.shape[1] * wide,
    )


def rest_product(before, vc, far, part):
    rows, wide = part.stop - part.start, far.shape[0]

    def kernel(b, w, a, out):
        for t in tiles(rows):
            at = slice(part.start + t.start, part.start + t.stop)
            out[t, :] = (b[at, :] + dot_nt(w[at, :], a[...])).astype(BF16)

    return call(
        kernel, "rest", [IN_VMEM] * 3, [stay(before), stay(vc), stay(far)], IN_VMEM, jax.ShapeDtypeStruct((rows, wide), BF16), [],
        2 * rows * vc.shape[1] * wide,
    )


def middle_product(own, other, cols, before):
    rows, wide = own.shape

    def kernel(m, r, c, *refs):
        for s in [slice(i, i + 256) for i in range(0, rows, 256)]:
            value = dot_nt(m[s, :], c[:, :wide]) + dot_nt(r[s, :], c[:, wide:])
            refs[-1][s, :] = value if before is None else value + refs[0][s, :]

    args = [stay(own), stay(other), stay(cols)] + ([] if before is None else [stay(before)])
    return call(
        kernel, "predicted", [IN_VMEM] * len(args), args, IN_VMEM, pltpu.VMEM((rows, cols.shape[0]), F32), [],
        4 * rows * cols.shape[0] * wide,
    )


def last_product(own, other, cols, before, out, part, rows):
    wide, depth = own.shape[1], cols.shape[0]
    spans = [slice(i, i + 256) for i in range(0, part.stop - part.start, 256)]
    slots = 4

    def kernel(m, r, c, *refs):
        to, held, sem = refs[-3:]
        moves = []
        for i, s in enumerate(spans):
            at = slice(part.start + s.start, part.start + s.stop)
            if i >= slots:
                moves[i - slots].wait()
            value = dot_nt(m[s, :], c[:, :wide]) + dot_nt(r[s, :], c[:, wide:])
            held[i % slots] = value if before is None else value + refs[0][at, :]
            moves.append(pltpu.make_async_copy(held.at[i % slots], to.at[at, :], sem.at[i % slots]))
            moves[i].start()
        for move in moves[-slots:]:
            move.wait()

    args = [stay(own), stay(other), stay(cols)] + ([] if before is None else [stay(before)])
    in_specs = [IN_VMEM] * len(args)
    aliases = {}
    if out is not None:
        aliases = {len(args): 0}
        args.append(leave(out))
        in_specs.append(IN_HBM)
    scratch = [pltpu.VMEM((slots, 256, depth), F32), pltpu.SemaphoreType.DMA((slots,))]
    return call(
        kernel, "predicted", in_specs, args, IN_HBM, jax.ShapeDtypeStruct((rows, depth), F32), scratch,
        4 * (part.stop - part.start) * depth * wide, aliases,
    )


def shards(nc, nt, affinity, comp_vectors, targ_vectors, comp_values, targ_values):
    cbits, tbits = nc.bit_length() - 1, nt.bit_length() - 2
    c_orders = ([1 << b for b in range(cbits)], [1 << b for b in reversed(range(cbits))])
    t_orders = ([2 << b for b in range(tbits)],) * 2
    iblock, jblock = comp_vectors.shape[1] // nc, targ_vectors.shape[1] // nt
    chunks = 2 if jblock % 256 == 0 else 1
    width = jblock // chunks

    def offset(position, order):
        return functools.reduce(lambda a, b: a ^ b, [mask for t, mask in enumerate(order) if (position >> (len(order) - 1 - t)) & 1], 0)

    def pick(orders, position, flip, core):
        return jnp.where(core == 0, offset(position, orders[flip]), offset(position, orders[1 - flip]))

    def c_blocks(p):
        return lax.axis_index("cmp") ^ pick(c_orders, p, 0, lax.axis_index("tgt") % 2)

    def keep(q):
        at = lax.axis_index("tgt")
        return at ^ pick(t_orders, q, 0, at % 2)

    def give(q):
        at = lax.axis_index("tgt")
        return at ^ 1 ^ pick(t_orders, q, 1, at % 2)

    def both(q):
        return keep(q) if q < nt // 2 else give(q - nt // 2)

    def swap_c(x, t):
        pairs = [(c * nt + i, (c ^ c_orders[i % 2][t]) * nt + i) for c in range(nc) for i in range(nt)]
        return lax.ppermute(x, ("cmp", "tgt"), pairs)

    def swap_t(x, t):
        return lax.ppermute(x, "tgt", [(i, i ^ t_orders[i % 2][t]) for i in range(nt)])

    def swap_core(x):
        return lax.ppermute(x, "tgt", [(i, i ^ 1) for i in range(nt)])

    bound = 6 * 0.0625 * 0.0546875 * affinity.shape[0] * nc * affinity.shape[1] * nt
    scale = 1.0
    while bound * scale > 65000:
        scale *= 0.5

    kinds = "c" * cbits + "t" * tbits
    steps = [(kind, kinds[:i].count(kind)) for i, kind in enumerate(kinds)]
    count = len(steps)

    def exchange(x, i):
        kind, t = steps[i]
        return swap_c(x, t) if kind == "c" else swap_t(x, t)

    def after(x, y):
        return lax.optimization_barrier((x, y))[0]

    every, upper, lower = slice(0, nt // 2), slice(nc // 2, nc), slice(0, nc // 2)
    give_cols = [(targ_vectors, give, jblock, k * width, width, every) for k in range(chunks)]
    keep_cols = [(targ_vectors, keep, jblock, k * width, width, every) for k in range(chunks)]
    if chunks == 2:
        sent, y, _, given = half_product(None, None, affinity, give_cols, BF16)
        came = [swap_core(sent)]
        sent, *kept = half_product(y, given, affinity, keep_cols, BF16)
        came.append(swap_core(sent))
        half, far, vc_far = keep_products(y, kept[0], came[0], None, comp_vectors, c_blocks, iblock, [upper], None, scale)
    else:
        sent, y, _, *kept = half_product(None, None, affinity, give_cols + keep_cols, BF16)
        came = [swap_core(sent)]
        half, far, vc_far, vc_near = keep_products(
            y, kept[0], came[0], None, comp_vectors, c_blocks, iblock, [upper, lower], None, scale
        )
    coming = [exchange(far.astype(F16), 0)]
    if chunks == 2:
        late_half, late_far, near, vc_near = keep_products(
            after(y, far), kept[1], came[1], vc_far, comp_vectors, c_blocks, iblock, [lower], half, scale
        )
    else:
        near, columns = near_product(half, vc_near, scale, targ_vectors, both, nt, [0], jblock, width)
    token, nears = near, [near]
    held = list(nears)
    rows = affinity.shape[0]
    total = out = begun = None

    def event(k, i, token):
        came = after(coming[k], token)
        if i == count - 1:
            n = came.shape[0] // 2
            came = jnp.concatenate([came[n:], came[:n]])
        if i < count:
            total = held[k] + came.astype(F32)
            if i < count - 2:
                n = total.shape[steps[i + 1][0] == "c"] // 2
                held[k], goes = (total[:, :n], total[:, n:]) if steps[i + 1][0] == "c" else (total[:n], total[n:])
            else:
                held[k] = goes = total
            if i < count - 1:
                goes = goes.astype(F16)
                coming[k] = exchange(goes, i + 1)
                return goes
            lt = lts[:, k * width : (k + 1) * width, None]
            total = total.reshape(2, width, -1) * (1 / scale) / (lt * comp_values[None, None, :] + 0.25)
            held[k] = total.astype(BF16).reshape(2 * width, -1)
        else:
            held[k] = jnp.concatenate([held[k], came], axis=int(steps[2 * count - 2 - i][0] == "c"))
        coming[k] = exchange(held[k], 2 * count - 3 - i)
        return held[k]

    final = 2 * count - 2
    token = event(0, 0, token)
    pair_values = swap_t(after(targ_values, token), tbits - 1)
    lts = jnp.stack([targ_values, pair_values])
    if chunks == 2:
        coming[0], lts = lax.optimization_barrier((coming[0], lts))
        token = event(0, 1, token)
        goes = after(late_far, token).astype(F16)
        coming.append(exchange(goes, 0))
        near, columns = near_product(after(late_half, goes), vc_near, scale, targ_vectors, both, nt, [0, 1], jblock, width)
        held.append(near)
    order = [(0, i) for i in range(chunks, final + 1)]
    if chunks == 2:
        late = [(1, i) for i in range(final + 1)]
        order = ORDER if count == 4 else [x for pair in zip(order + [None], late) for x in pair if x]
    whole, parts = [slice(0, rows)], [slice(0, rows // 2), slice(rows // 2, rows)]
    for k, i in order:
        if i < final:
            token = event(k, i, token)
            if (k, i) == (chunks - 1, final - 1) and chunks > 1:
                early, _ = lax.optimization_barrier((early, token))
                other = swap_core(early)
                other, begun = lax.optimization_barrier((other, part_product(vc_near, held[k])))
                total = token = middle_product(early, other, columns[0], None)
        else:
            last = after(coming[k], token)
            if k < chunks - 1:
                mapped = [mapped_product(vc_near, vc_far, held[k], last, s) for s in whole]
            else:
                begun = part_product(vc_near, held[k]) if begun is None else begun
                mapped = [rest_product(begun, vc_far, last, s) for s in parts]
            early = token = mapped[0]
    for x, s in zip(mapped, parts):
        out = last_product(x, swap_core(x), columns[chunks - 1], total, out, s, rows)
    return out


def solution(mesh):
    in_specs = (P("cmp", "tgt"), P("cmp", None), P("tgt", None), P("cmp"), P("tgt"))
    out_specs = P("cmp", "tgt")
    body = functools.partial(shards, mesh.shape["cmp"], mesh.shape["tgt"])
    return jax.shard_map(body, mesh=mesh, in_specs=in_specs, out_specs=out_specs, check_vma=False)
```
